512 devices in a mesh: row: 32 (over z_hi, y), col: 16 (over z_lo, x, core).
Axes of the slice: x: 4, y: 8, z: 8 (z_hi: 4, z_lo: 2; z = z_hi * 2 + z_lo), core: 2. Of those that a mesh axis runs over, the one named last changes fastest.
Arguments:
- probes: bfloat16 [524288, 64], P(('row', 'col')), may hold values from -2 to 2
- points: bfloat16 [3, 524288], P(None, ('row', 'col')), may hold values from 0 to 1
- skeleton: bfloat16 [3, 229376], P(None, ('row', 'col')), may hold values from 0 to 1
- leaf_basis: bfloat16 [524288, 64], P(('row', 'col')), may hold values from -0.375 to 0.375
- transfer: bfloat16 [196608, 64], P(('row', 'col')), may hold values from -0.75 to 0.75
- near_list: int32 [32, 16, 2, 64], P('row', 'col'), may hold values from 0 to 127, as said below
- near_count: int32 [32, 16], P('row', 'col'), may hold values from 8 to 64, as said below
- far_list: int32 [32, 16, 2, 128], P('row', 'col'), may hold values from 0 to 223, as said below
- far_count: int32 [32, 16], P('row', 'col'), may hold values from 16 to 128, as said below
Outputs:
- sample: bfloat16 [524288, 64], P(('row', 'col'))
The draws below stay inside these ranges and needn't reach their ends.
Inputs may be any that keep to these rules, and one draw needn't show every extreme that they name: `near_list`: row entries index the 64 row leaves of the device's row, column entries the 128 column leaves of its column; only the first near_count slots are used. `near_count`: used slots of one device: 64 on some device in every draw, else 64/2, /4 or /8. `far_list`: row entries index the 112 row clusters, column entries the 224 column clusters; both clusters of a slot lie on the same level; only the first far_count slots are used. `far_count`: used slots of one device: 128 on some device in every draw, else 128/2, /4 or /8.
All inputs are finite; a program needn't handle non-finite values.
Results may differ from the reference program's by a relative error of at most 0.02.
Values may be sent and summed in bfloat16 or wider, within the bound.
A program may use at most 64 MiB of HBM per device.

```python
import math
import jax
import jax.numpy as jnp
from jax import lax

LEAF = 256
RANK = 64
SAMPLES = 64
NEAR_MOST = 64
FAR_MOST = 128
NPTS = 524288
CLUSTERS = 3584
N_ROW = 32
N_COL = 16
DEVICES = 512


def live_counts(key, most):
    first, second = jax.random.split(key)
    shifts = jax.random.randint(first, (N_ROW * N_COL,), 0, 4)
    counts = jnp.right_shift(jnp.full((N_ROW * N_COL,), most, jnp.int32), shifts)
    chosen = jax.random.randint(second, (), 0, N_ROW * N_COL)
    counts = counts.at[chosen].set(most)
    return counts.reshape(N_ROW, N_COL)


def draw_near_count(key, part):
    key = jax.random.fold_in(key, 11)
    return live_counts(key, NEAR_MOST)


def draw_far_count(key, part):
    key = jax.random.fold_in(key, 13)
    return live_counts(key, FAR_MOST)


def draw_near_list(key, part):
    key = jax.random.fold_in(key, 17)
    first, second = jax.random.split(key)
    shape = (N_ROW, N_COL, 1, NEAR_MOST)
    targets = jax.random.randint(first, shape, 0, 4 * N_COL)
    sources = jax.random.randint(second, shape, 0, 4 * N_ROW)
    return jnp.concatenate([targets, sources], axis=2).astype(jnp.int32)


def draw_far_list(key, part):
    key = jax.random.fold_in(key, 19)
    keys = jax.random.split(key, 5)
    shape = (N_ROW, N_COL, 1, FAR_MOST)
    level = jax.random.randint(keys[0], shape, 0, 3)
    offset = jnp.where(level == 0, 0, jnp.where(level == 1, 4, 6))
    span = jnp.right_shift(jnp.full(shape, 4, jnp.int32), level)
    target_dev = jax.random.randint(keys[1], shape, 0, N_COL)
    target_local = jax.random.randint(keys[2], shape, 0, 4) % span
    source_dev = jax.random.randint(keys[3], shape, 0, N_ROW)
    source_local = jax.random.randint(keys[4], shape, 0, 4) % span
    targets = target_dev * 7 + offset + target_local
    sources = source_dev * 7 + offset + source_local
    return jnp.concatenate([targets, sources], axis=2).astype(jnp.int32)


def steps_of(key, shape, shards, least, high):
    def one(dim, blocks):
        steps = jax.random.uniform(jax.random.fold_in(jax.random.fold_in(key, 6), dim), (blocks,), jnp.float32, least / len(shards), high / len(shards))
        return jnp.repeat(jnp.exp(steps), shape[dim] // blocks).reshape((-1,) + (1,) * (len(shape) - dim - 1))

    factor_of = one(*shards[0])
    for cut in shards[1:]:
        factor_of = factor_of * one(*cut)
    return factor_of


def bell_draw(own_key, dims, deviation, bound, cuts=(), held_as=jnp.bfloat16):
    loudness = steps_of(own_key, dims, cuts, -0.22, 0.18) if cuts else 1.0
    array = jax.random.normal(own_key, dims, jnp.float32) * deviation * loudness
    return jnp.minimum(jnp.maximum(array, -bound), bound).astype(held_as)


def setup_inputs(seed: int = 0) -> dict:
    key_of = jax.random.split(jax.random.key(seed), 10)
    probes = bell_draw(key_of[0], (NPTS, SAMPLES), 0.25, 2.0, ((0, 512),))
    points = jnp.clip(1.0 * jax.random.uniform(key_of[1], (3, NPTS), jnp.float32) ** steps_of(key_of[1], (3, NPTS), ((1, 512),), -0.2, 0.2), 0.0, 1.0).astype(jnp.bfloat16)
    skeleton = jnp.clip(1.0 * jax.random.uniform(key_of[2], (3, CLUSTERS * RANK), jnp.float32) ** steps_of(key_of[2], (3, CLUSTERS * RANK), ((1, 512),), -0.2, 0.2), 0.0, 1.0).astype(jnp.bfloat16)
    leaf_basis = bell_draw(key_of[3], (NPTS, RANK), LEAF ** -0.5, 0.375, ((0, 512),))
    transfer = bell_draw(key_of[4], (6 * DEVICES * RANK, RANK), RANK ** -0.5, 0.75, ((0, 512),))
    near_list = draw_near_list(jax.random.fold_in(key_of[9], 71), 0)
    near_count = draw_near_count(jax.random.fold_in(key_of[9], 71), 0)
    far_list = draw_far_list(jax.random.fold_in(key_of[9], 71), 0)
    far_count = draw_far_count(jax.random.fold_in(key_of[9], 71), 0)
    return dict(probes=probes, points=points, skeleton=skeleton, leaf_basis=leaf_basis, transfer=transfer, near_list=near_list, near_count=near_count, far_list=far_list, far_count=far_count)


length_scale = 0.15
root_three = math.sqrt(3.0)

def rounded(values):
    return lax.optimization_barrier(values.astype(jnp.bfloat16)).astype(jnp.float32)

def matern(first, second):
    first = first.astype(jnp.float32)
    second = second.astype(jnp.float32)
    dist = jnp.zeros(first.shape[1:] + second.shape[-1:], jnp.float32)
    for axis in range(3):
        gap = first[axis][..., :, None] - second[axis][..., None, :]
        dist = dist + gap * gap
    scaled = root_three * jnp.sqrt(dist) / length_scale
    return (1.0 + scaled) * jnp.exp(-scaled)

def upward(probe_rows, basis_rows, move_rows):
    leaf = jnp.einsum('klr,kls->krs', basis_rows.reshape(4, LEAF, RANK).astype(jnp.float32), probe_rows.reshape(4, LEAF, SAMPLES).astype(jnp.float32))
    leaf = leaf.astype(jnp.bfloat16)
    moves = move_rows.reshape(6, RANK, RANK).astype(jnp.float32)
    middle = jnp.einsum('kap,kas->kps', moves[0:4], leaf.astype(jnp.float32))
    middle = middle.reshape(2, 2, RANK, SAMPLES).sum(axis=1).astype(jnp.bfloat16)
    upper = jnp.einsum('kap,kas->kps', moves[4:6], middle.astype(jnp.float32))
    upper = upper.sum(axis=0, keepdims=True).astype(jnp.bfloat16)
    return jnp.concatenate([leaf, middle, upper], axis=0)

def near_terms(row_points, col_points, col_probes, pairs, live, groups):
    row_leaves = row_points.reshape(3, -1, LEAF)
    col_leaves = col_points.reshape(3, -1, LEAF)
    col_values = col_probes.reshape(-1, LEAF, SAMPLES)
    totals = jnp.zeros((row_leaves.shape[1], LEAF, SAMPLES), jnp.float32)

    def step(group, totals):
        slots = lax.dynamic_slice_in_dim(pairs, group * 4, 4, 1)
        alive = group * 4 + jnp.arange(4, dtype=jnp.int32) < live
        targets = slots[0]
        sources = slots[1]
        kernel = rounded(matern(row_leaves[:, targets], col_leaves[:, sources]))
        values = col_values[sources].astype(jnp.float32)
        term = jnp.einsum('gab,gbs->gas', kernel, values)
        term = jnp.where(alive[:, None, None], term, 0.0)
        return totals.at[targets].add(term)
    totals = lax.fori_loop(0, groups, step, totals)
    return totals.reshape(-1, SAMPLES)

def far_terms(row_skel, col_skel, col_coeffs, pairs, live, groups):
    row_sets = row_skel.reshape(3, -1, RANK)
    col_sets = col_skel.reshape(3, -1, RANK)
    totals = jnp.zeros((row_sets.shape[1], RANK, SAMPLES), jnp.float32)

    def step(group, totals):
        slots = lax.dynamic_slice_in_dim(pairs, group * 16, 16, 1)
        alive = group * 16 + jnp.arange(16, dtype=jnp.int32) < live
        targets = slots[0]
        sources = slots[1]
        kernel = rounded(matern(row_sets[:, targets], col_sets[:, sources]))
        values = col_coeffs[sources].astype(jnp.float32)
        term = jnp.einsum('gab,gbs->gas', kernel, values)
        term = jnp.where(alive[:, None, None], term, 0.0)
        return totals.at[targets].add(term)
    return lax.fori_loop(0, groups, step, totals)

def descend(far_total, moves):
    moves = moves.astype(jnp.float32)
    upper = far_total[:, 6]
    middle = far_total[:, 4:6] + jnp.einsum('dkab,dbs->dkas', moves[:, 4:6], upper, precision=lax.Precision.HIGHEST)
    spread = jnp.repeat(middle, 2, axis=1)
    return far_total[:, 0:4] + jnp.einsum('dkab,dkbs->dkas', moves[:, 0:4], spread, precision=lax.Precision.HIGHEST)

def reference(probes, points, skeleton, leaf_basis, transfer, near_list, near_count, far_list, far_count):
    probes_dev = probes.reshape(N_ROW, N_COL, 4 * LEAF, SAMPLES)
    basis_dev = leaf_basis.reshape(N_ROW, N_COL, 4 * LEAF, RANK)
    moves_dev = transfer.reshape(N_ROW, N_COL, 6 * RANK, RANK)
    coeffs = jax.vmap(jax.vmap(upward))(probes_dev, basis_dev, moves_dev)
    points_dev = points.reshape(3, N_ROW, N_COL, 4 * LEAF)
    skel_dev = skeleton.reshape(3, N_ROW, N_COL, 7 * RANK)
    column_side = (jnp.moveaxis(probes_dev, 1, 0).reshape(N_COL, N_ROW * 4 * LEAF, SAMPLES), jnp.moveaxis(points_dev, 2, 0).reshape(N_COL, 3, N_ROW * 4 * LEAF), jnp.moveaxis(skel_dev, 2, 0).reshape(N_COL, 3, N_ROW * 7 * RANK), jnp.moveaxis(coeffs, 1, 0).reshape(N_COL, N_ROW * 7, RANK, SAMPLES))

    def one_row(inputs):
        row_points, row_skel, near_pairs, near_live, far_pairs, far_live, basis_rows, move_rows = inputs

        def one_device(carry, items):
            near_total, far_total = carry
            col_probes, col_points, col_skel, col_coeffs, n_pairs, n_live, f_pairs, f_live = items
            near_part = near_terms(row_points, col_points, col_probes, n_pairs, n_live, (n_live + 3) // 4)
            far_part = far_terms(row_skel, col_skel, col_coeffs, f_pairs, f_live, (f_live + 15) // 16)
            return ((near_total + rounded(near_part), far_total + far_part), None)
        start = (jnp.zeros((N_COL * 4 * LEAF, SAMPLES), jnp.float32), jnp.zeros((N_COL * 7, RANK, SAMPLES), jnp.float32))
        (near_total, far_total), unused = lax.scan(one_device, start, column_side + (near_pairs, near_live, far_pairs, far_live))
        leaf_far = descend(far_total.reshape(N_COL, 7, RANK, SAMPLES), move_rows.reshape(N_COL, 6, RANK, RANK))
        expanded = jnp.einsum('dklr,dkrs->dkls', basis_rows.reshape(N_COL, 4, LEAF, RANK).astype(jnp.float32), leaf_far, precision=lax.Precision.HIGHEST)
        return (near_total.reshape(N_COL, 4, LEAF, SAMPLES) + expanded).astype(jnp.bfloat16)
    rows = lax.map(one_row, (jnp.moveaxis(points_dev, 1, 0).reshape(N_ROW, 3, N_COL * 4 * LEAF), jnp.moveaxis(skel_dev, 1, 0).reshape(N_ROW, 3, N_COL * 7 * RANK), near_list, near_count, far_list, far_count, basis_dev, moves_dev))
    return rows.reshape(N_ROW * N_COL * 4 * LEAF, SAMPLES)
```

```python
import math

import jax
import jax.numpy as jnp
import numpy as np
from jax import lax
from jax.experimental import pallas as pl
from jax.experimental.pallas import tpu as pltpu
from jax.sharding import PartitionSpec as P

LEAF = 256
RANK = 64
SAMPLES = 64
N_ROW = 32
N_COL = 16
N_Y = 8
N_ZH = 4
NEAR_MOST = 64
FAR_MOST = 128
PACK = 640
MESH = pl.DeviceIdType.MESH
F32 = jnp.float32
BF16 = jnp.bfloat16
RATE = math.sqrt(3.0) / 0.15
RATE2 = RATE * math.log2(math.e)


def dot_t(a, b):
    return lax.dot_general(a, b, (((1,), (1,)), ((), ())), preferred_element_type=F32)


def dot_l(a, b):
    return lax.dot_general(a, b, (((0,), (0,)), ((), ())), preferred_element_type=F32)


def dot_n(a, b):
    return jnp.dot(a, b, preferred_element_type=F32)


def selections():
    col = np.zeros((4, 16, 32), np.float32)
    row = np.zeros((4, 16, 32), np.float32)
    for k in range(4):
        for i in range(3):
            col[k, i, i * 4 + k] = -2.0
            row[k, i, i * 4 + k] = 1.0
            col[k, 3 + i, 16 + 4 * i + k] = 1.0
            row[k, 3 + i, 28] = 1.0
            col[k, 6 + i, 28] = 1.0
            row[k, 6 + i, 16 + 4 * i + k] = 1.0
    return np.concatenate([col.reshape(64, 32), row.reshape(64, 32)], axis=0)


def coordinates(points, skeleton):
    pts = points.reshape(12, LEAF)
    skel = jnp.pad(skeleton, ((0, 0), (0, 64))).reshape(12, 128)
    zero = jnp.zeros((4, 128), BF16)
    return jnp.concatenate(
        [pts[:, :128], zero, pts[:, 128:], zero, skel, zero, jnp.zeros((16, 128), BF16)], axis=0
    )


def upward_packet(probes_t, basis_t, moves_t):
    leaves = [
        dot_t(probes_t[:, k * LEAF : (k + 1) * LEAF], basis_t[:, k * LEAF : (k + 1) * LEAF])
        for k in range(4)
    ]
    leaf = jnp.concatenate(leaves, axis=1).astype(BF16)
    mids = [
        dot_t(leaf[:, j * 128 : (j + 1) * 128], moves_t[:, j * 128 : (j + 1) * 128])
        for j in range(2)
    ]
    mid = jnp.concatenate(mids, axis=1).astype(BF16)
    top = dot_t(mid, moves_t[:, 256:384]).astype(BF16)
    return jnp.concatenate([leaf, mid, top, jnp.zeros((64, 64), BF16)], axis=1)


def gather_kernel(
    probes_any, probes_t, basis_t, moves_t, geo, all_p, all_q, all_g,
    pack, send, recv_p, recv_q, recv_g, local_sem,
):
    r = lax.axis_index("row")
    c = lax.axis_index("col")
    zh = r // N_Y
    y = r % N_Y
    up = ((zh + 1) % N_ZH) * N_Y + y
    down = ((zh + 3) % N_ZH) * N_Y + y
    right = zh * N_Y + (y + 1) % N_Y
    left = zh * N_Y + (y + 7) % N_Y

    def slot(dz, dy):
        return ((zh + dz) % N_ZH) * N_Y + (y + dy) % N_Y

    barrier = pltpu.get_barrier_semaphore()
    for row in (up, down, right, left):
        pl.semaphore_signal(barrier, inc=1, device_id=(row, c), device_id_type=MESH)

    @pl.loop(1, N_COL)
    def _(d):
        pl.semaphore_signal(
            barrier, inc=1, device_id=(r, (c + d) % N_COL), device_id_type=MESH
        )

    pack[:, 0:512] = upward_packet(probes_t[...], basis_t[...], moves_t[...])
    pack[:, 512:640] = geo[...]
    pl.semaphore_wait(barrier, 4 + N_COL - 1)

    sends = []

    def copy(src, dst, sem, row):
        one = pltpu.make_async_remote_copy(
            src_ref=src, dst_ref=dst, send_sem=send.at[len(sends)], recv_sem=sem,
            device_id=(row, c), device_id_type=MESH,
        )
        one.start()
        sends.append(one)

    def arrived(dst, sem):
        pltpu.make_async_remote_copy(
            src_ref=dst, dst_ref=dst, send_sem=send.at[0], recv_sem=sem,
            device_id=(r, c), device_id_type=MESH,
        ).wait_recv()

    halves = (pl.ds(0, 32), pl.ds(32, 32))

    def mover(buf, sems):
        def push(s, row, src=None):
            copy(buf.at[s] if src is None else src, buf.at[s], sems.at[s, 0], row)

        def push_half(s, h, row):
            copy(buf.at[s, halves[h]], buf.at[s, halves[h]], sems.at[s, h], row)

        def wait(s):
            arrived(buf.at[s], sems.at[s, 0])

        def wait_half(s, h):
            arrived(buf.at[s, halves[h]], sems.at[s, h])

        return push, push_half, wait, wait_half

    p_push, p_push_half, p_wait, p_wait_half = mover(all_p, recv_p)
    q_push, q_push_half, q_wait, q_wait_half = mover(all_q, recv_q)
    me = slot(0, 0)

    q_push(me, right, pack)
    q_push(me, left, pack)
    p_push(me, up, probes_any)
    p_push(me, down, probes_any)
    p_push(me, right, probes_any)
    p_push(me, left, probes_any)
    q_push(me, up, pack)
    q_push(me, down, pack)

    @pl.loop(1, N_COL)
    def _(d):
        pltpu.make_async_remote_copy(
            src_ref=pack.at[:, pl.ds(512, 128)], dst_ref=all_g.at[c],
            send_sem=recv_g.at[0, d], recv_sem=recv_g.at[1, d],
            device_id=(r, (c + d) % N_COL), device_id_type=MESH,
        ).start()

    own = [
        pltpu.make_async_copy(probes_any, all_p.at[me], local_sem.at[0]),
        pltpu.make_async_copy(pack, all_q.at[me], local_sem.at[1]),
        pltpu.make_async_copy(pack.at[:, pl.ds(512, 128)], all_g.at[c], local_sem.at[2]),
    ]
    for one in own:
        one.start()

    p_wait(slot(3, 0))
    p_push_half(slot(3, 0), 0, up)
    p_wait(slot(1, 0))
    p_push_half(slot(1, 0), 1, down)
    for dz in (3, 1):
        p_push(slot(dz, 0), right)
        p_push(slot(dz, 0), left)
    p_wait_half(slot(2, 0), 0)
    p_wait_half(slot(2, 0), 1)
    p_push(slot(2, 0), right)
    p_push(slot(2, 0), left)

    def q_z_forward(dy):
        q_wait(slot(3, dy))
        q_push_half(slot(3, dy), 0, up)
        q_wait(slot(1, dy))
        q_push_half(slot(1, dy), 1, down)

    q_z_forward(0)
    for k in (1, 2, 3):
        q_wait(slot(0, -k))
        if k < 3:
            q_push(slot(0, -k), right)
        else:
            q_push_half(slot(0, -k), 0, right)
        q_wait(slot(0, k))
        if k < 3:
            q_push(slot(0, k), left)
        else:
            q_push_half(slot(0, k), 1, left)
        for dy in (-k, k):
            q_push(slot(0, dy), up)
            q_push(slot(0, dy), down)
        for dz in (0, 3, 1, 2):
            p_wait(slot(dz, -k))
            if k < 3:
                p_push(slot(dz, -k), right)
            else:
                p_push_half(slot(dz, -k), 0, right)
            p_wait(slot(dz, k))
            if k < 3:
                p_push(slot(dz, k), left)
            else:
                p_push_half(slot(dz, k), 1, left)
        if k == 3:
            q_wait_half(slot(0, 4), 0)
            q_wait_half(slot(0, 4), 1)
            q_push(slot(0, 4), up)
            q_push(slot(0, 4), down)
        for dy in (-k, k):
            q_z_forward(dy)
    q_z_forward(4)
    for dz in (0, 3, 1, 2):
        p_wait_half(slot(dz, 4), 0)
        p_wait_half(slot(dz, 4), 1)
    for dy in (0, -1, 1, -2, 2, -3, 3, 4):
        q_wait_half(slot(2, dy), 0)
        q_wait_half(slot(2, dy), 1)

    @pl.loop(1, N_COL)
    def _(d):
        pltpu.make_async_remote_copy(
            src_ref=pack.at[:, pl.ds(512, 128)], dst_ref=all_g.at[(c + N_COL - d) % N_COL],
            send_sem=recv_g.at[0, d], recv_sem=recv_g.at[1, d],
            device_id=(r, (c + d) % N_COL), device_id_type=MESH,
        ).wait()

    for one in own:
        one.wait()
    for one in sends:
        one.wait_send()


def gather(probes_t, basis_t, moves_t, geo):
    vmem = pl.BlockSpec(memory_space=pltpu.VMEM)
    anywhere = pl.BlockSpec(memory_space=pl.ANY)
    return pl.pallas_call(
        gather_kernel,
        out_shape=(
            jax.ShapeDtypeStruct((N_ROW, 64, 1024), BF16),
            jax.ShapeDtypeStruct((N_ROW, 64, PACK), BF16),
            jax.ShapeDtypeStruct((N_COL, 64, 128), BF16),
        ),
        in_specs=[anywhere, vmem, vmem, vmem, vmem],
        out_specs=(anywhere, anywhere, anywhere),
        scratch_shapes=[
            pltpu.VMEM((64, PACK), BF16),
            pltpu.SemaphoreType.DMA((80,)),
            pltpu.SemaphoreType.DMA((N_ROW, 2)),
            pltpu.SemaphoreType.DMA((N_ROW, 2)),
            pltpu.SemaphoreType.DMA((2, N_COL)),
            pltpu.SemaphoreType.DMA((3,)),
        ],
        compiler_params=pltpu.CompilerParams(
            collective_id=0, has_side_effects=True, vmem_limit_bytes=32 << 20
        ),
        name="gather",
    )(probes_t, probes_t, basis_t, moves_t, geo)


def features(sel, geo):
    flat = jnp.concatenate([geo[0:16], geo[16:32], geo[32:48]], axis=1).astype(F32)
    squares = flat * flat
    norm = squares[0:4] + squares[4:8] + squares[8:12]
    high = norm.astype(BF16).astype(F32)
    rest = norm - high
    middle = rest.astype(BF16).astype(F32)
    low = rest - middle
    stack = jnp.concatenate([flat, high, middle, low, jnp.ones_like(norm)], axis=0)
    return dot_n(sel, stack.astype(BF16)).astype(BF16)


def matern(square):
    square = jnp.maximum(square, 1e-30)
    dist = square * lax.rsqrt(square)
    return ((1.0 + RATE * dist) * jnp.exp2(dist * (-RATE2))).astype(BF16)


def blocks_kernel(
    near_list, near_count, far_list, far_count, sel, all_p, all_q, all_g, near_out, far_out,
    col_leaf, row_leaf, col_skel, row_skel, coeffs, near_acc, far_acc,
):
    @pl.loop(0, N_ROW)
    def _(d):
        feat = features(sel[0:64], all_q[d, :, 512:640])
        col_leaf[pl.ds(d * 4, 4)] = feat[:, 0:256].reshape(4, 16, 256)
        for j in range(7):
            half = feat[(j // 2) * 16 : (j // 2) * 16 + 16, 256 + (j % 2) * 64 : 320 + (j % 2) * 64]
            col_skel[d * 7 + j] = half
            coeffs[d * 7 + j] = all_q[d, :, j * 64 : (j + 1) * 64]

    @pl.loop(0, N_COL)
    def _(d):
        feat = features(sel[64:128], all_g[d])
        row_leaf[pl.ds(d * 4, 4)] = feat[:, 0:256].reshape(4, 16, 256)
        for j in range(7):
            half = feat[(j // 2) * 16 : (j // 2) * 16 + 16, 256 + (j % 2) * 64 : 320 + (j % 2) * 64]
            row_skel[d * 7 + j] = half

    near_acc[...] = jnp.zeros_like(near_acc)
    far_acc[...] = jnp.zeros_like(far_acc)

    @pl.loop(0, near_count[0, 0] // 2)
    def _(g):
        for u in range(2):
            a = near_list[0, g * 2 + u]
            b = near_list[1, g * 2 + u]
            kern = matern(dot_l(col_leaf[b], row_leaf[a]))
            lanes = pl.ds(pl.multiple_of((b % 4) * LEAF, LEAF), LEAF)
            near_acc[a] += dot_n(all_p[b // 4, :, lanes], kern)

    @pl.loop(0, far_count[0, 0] // 8)
    def _(g):
        for u in range(8):
            a = far_list[0, g * 8 + u]
            b = far_list[1, g * 8 + u]
            kern = matern(dot_l(col_skel[b], row_skel[a]))
            far_acc[a] += dot_n(coeffs[b], kern)

    @pl.loop(0, N_COL)
    def _(d):
        for k in range(4):
            near_out[d, :, k * LEAF : (k + 1) * LEAF] = near_acc[d * 4 + k].astype(BF16)
        for j in range(4):
            low = far_acc[d * 7 + 2 * j]
            high = far_acc[d * 7 + 2 * j + 1] if j < 3 else jnp.zeros((64, 64), F32)
            far_out[d, :, j * 128 : (j + 1) * 128] = jnp.concatenate([low, high], axis=1).astype(BF16)


def blocks(near_list, near_count, far_list, far_count, sel, all_p, all_q, all_g):
    vmem = pl.BlockSpec(memory_space=pltpu.VMEM)
    smem = pl.BlockSpec(memory_space=pltpu.SMEM)
    return pl.pallas_call(
        blocks_kernel,
        out_shape=(
            jax.ShapeDtypeStruct((N_COL, 64, 1024), BF16),
            jax.ShapeDtypeStruct((N_COL, 64, 512), BF16),
        ),
        in_specs=[smem, smem, smem, smem, vmem, vmem, vmem, vmem],
        out_specs=(vmem, vmem),
        scratch_shapes=[
            pltpu.VMEM((4 * N_ROW, 16, LEAF), BF16),
            pltpu.VMEM((4 * N_COL, 16, LEAF), BF16),
            pltpu.VMEM((7 * N_ROW, 16, RANK), BF16),
            pltpu.VMEM((7 * N_COL, 16, RANK), BF16),
            pltpu.VMEM((7 * N_ROW, SAMPLES, RANK), BF16),
            pltpu.VMEM((4 * N_COL, SAMPLES, LEAF), F32),
            pltpu.VMEM((7 * N_COL, SAMPLES, RANK), F32),
        ],
        compiler_params=pltpu.CompilerParams(vmem_limit_bytes=48 << 20),
        name="blocks",
    )(near_list, near_count, far_list, far_count, sel, all_p, all_q, all_g)


def split_dot(a, b):
    high = a.astype(BF16)
    low = (a - high.astype(F32)).astype(BF16)
    both = dot_n(jnp.concatenate([high, low], axis=0), b)
    return both[: a.shape[0]] + both[a.shape[0] :]


def reduce_kernel(
    near, far, basis_t, moves_t, out,
    near_sib, far_sib, near_sum, far_sum, near_in, far_in, sems, sib_sems,
):
    r = lax.axis_index("row")
    c = lax.axis_index("col")
    core = c % 2
    chip = c // 2
    sibling = chip * 2 + 1 - core

    barrier = pltpu.get_barrier_semaphore()
    pl.semaphore_signal(barrier, inc=1, device_id=(r, sibling), device_id_type=MESH)

    @pl.loop(1, 8)
    def _(d):
        other = ((chip + d) % 8) * 2 + core
        pl.semaphore_signal(barrier, inc=1, device_id=(r, other), device_id_type=MESH)

    pl.semaphore_wait(barrier, 8)

    def sib_copy(d, src_chip):
        theirs = src_chip * 2 + 1 - core
        return (
            pltpu.make_async_remote_copy(
                src_ref=near.at[theirs], dst_ref=near_sib.at[d],
                send_sem=sib_sems.at[0, d], recv_sem=sib_sems.at[1, d],
                device_id=(r, sibling), device_id_type=MESH,
            ),
            pltpu.make_async_remote_copy(
                src_ref=far.at[theirs], dst_ref=far_sib.at[d],
                send_sem=sib_sems.at[2, d], recv_sem=sib_sems.at[3, d],
                device_id=(r, sibling), device_id_type=MESH,
            ),
        )

    def chip_copy(d):
        other = ((chip + d) % 8) * 2 + core
        return (
            pltpu.make_async_remote_copy(
                src_ref=near_sum.at[d], dst_ref=near_in.at[d],
                send_sem=sems.at[0, d], recv_sem=sems.at[1, d],
                device_id=(r, other), device_id_type=MESH,
            ),
            pltpu.make_async_remote_copy(
                src_ref=far_sum.at[d], dst_ref=far_in.at[d],
                send_sem=sems.at[2, d], recv_sem=sems.at[3, d],
                device_id=(r, other), device_id_type=MESH,
            ),
        )

    @pl.loop(0, 8)
    def _(i):
        d = 7 - i
        for one in sib_copy(d, (chip + d) % 8):
            one.start()

    @pl.loop(0, 7)
    def _(i):
        d = 7 - i
        for one in sib_copy(d, (chip + d) % 8):
            one.wait_recv()
        mine = ((chip + d) % 8) * 2 + core
        near_sum[d] = (near[mine].astype(F32) + near_sib[d].astype(F32)).astype(BF16)
        far_sum[d] = (far[mine].astype(F32) + far_sib[d].astype(F32)).astype(BF16)
        for one in chip_copy(d):
            one.start()

    for one in sib_copy(0, chip):
        one.wait_recv()
    near_total = near[c].astype(F32) + near_sib[0].astype(F32)
    far_total = far[c].astype(F32) + far_sib[0].astype(F32)
    near_keep = near_total
    for d in range(1, 8):
        for one in chip_copy(d):
            one.wait_recv()
        near_keep = near_keep + near_in[d].astype(F32)
        far_total = far_total + far_in[d].astype(F32)

    top = far_total[:, 384:448]
    middle = far_total[:, 256:384] + split_dot(top, moves_t[:, 256:384])
    for k in range(4):
        leaf = far_total[:, k * 64 : (k + 1) * 64] + split_dot(
            middle[:, (k // 2) * 64 : (k // 2) * 64 + 64], moves_t[:, k * 64 : (k + 1) * 64]
        )
        lanes = slice(k * LEAF, (k + 1) * LEAF)
        out[:, lanes] = (near_keep[:, lanes] + split_dot(leaf, basis_t[:, lanes])).astype(BF16)

    @pl.loop(0, 8)
    def _(d):
        for one in sib_copy(d, (chip + d) % 8):
            one.wait_send()

    @pl.loop(1, 8)
    def _(d):
        for one in chip_copy(d):
            one.wait_send()


def reduce(near, far, basis_t, moves_t):
    vmem = pl.BlockSpec(memory_space=pltpu.VMEM)
    return pl.pallas_call(
        reduce_kernel,
        out_shape=jax.ShapeDtypeStruct((64, 1024), BF16),
        in_specs=[vmem, vmem, vmem, vmem],
        out_specs=vmem,
        scratch_shapes=[
            pltpu.VMEM((8, 64, 1024), BF16),
            pltpu.VMEM((8, 64, 512), BF16),
            pltpu.VMEM((8, 64, 1024), BF16),
            pltpu.VMEM((8, 64, 512), BF16),
            pltpu.VMEM((8, 64, 1024), BF16),
            pltpu.VMEM((8, 64, 512), BF16),
            pltpu.SemaphoreType.DMA((4, 8)),
            pltpu.SemaphoreType.DMA((4, 8)),
        ],
        compiler_params=pltpu.CompilerParams(
            collective_id=1, has_side_effects=True, vmem_limit_bytes=32 << 20
        ),
        name="reduce",
    )(near, far, basis_t, moves_t)


def local(
    probes, points, skeleton, leaf_basis, transfer, near_list, near_count, far_list, far_count
):
    probes_t, basis_t, moves_t = probes.T, leaf_basis.T, transfer.T
    sel = jnp.asarray(selections(), BF16)
    geo = coordinates(points, skeleton)
    all_p, all_q, all_g = gather(probes_t, basis_t, moves_t, geo)
    near, far = blocks(
        near_list[0, 0], near_count, far_list[0, 0], far_count, sel, all_p, all_q, all_g
    )
    return reduce(near, far, basis_t, moves_t).T


def solution(mesh):
    placed = (
        P(("row", "col"), None),
        P(None, ("row", "col")),
        P(None, ("row", "col")),
        P(("row", "col"), None),
        P(("row", "col"), None),
        P("row", "col", None, None),
        P("row", "col"),
        P("row", "col", None, None),
        P("row", "col"),
    )
    return jax.shard_map(
        local, mesh=mesh, in_specs=placed, out_specs=P(("row", "col"), None), check_vma=False
    )
```

```python
import functools
import math

import jax
import jax.numpy as jnp
import numpy as np
from jax import lax
from jax.experimental import pallas as pl
from jax.experimental.pallas import tpu as pltpu
from jax.sharding import PartitionSpec as P

LEAF = 256
RANK = 64
SAMPLES = 64
N_ROW = 32
N_COL = 16
N_Y = 8
N_ZH = 4
NEAR_MOST = 64
FAR_MOST = 128
GEO = 384
MESH = pl.DeviceIdType.MESH
F32 = jnp.float32
BF16 = jnp.bfloat16
RATE = math.sqrt(3.0) / 0.15
RATE2 = RATE * math.log2(math.e)


def dot_t(a, b):
    return lax.dot_general(a, b, (((1,), (1,)), ((), ())), preferred_element_type=F32)


def dot_l(a, b):
    return lax.dot_general(a, b, (((0,), (0,)), ((), ())), preferred_element_type=F32)


def dot_n(a, b):
    return jnp.dot(a, b, preferred_element_type=F32)


def selections():
    col = np.zeros((4, 16, 32), np.float32)
    row = np.zeros((4, 16, 32), np.float32)
    for k in range(4):
        for i in range(3):
            col[k, i, i * 4 + k] = -2.0
            row[k, i, i * 4 + k] = 1.0
            col[k, 3 + i, 16 + 4 * i + k] = 1.0
            row[k, 3 + i, 28] = 1.0
            col[k, 6 + i, 28] = 1.0
            row[k, 6 + i, 16 + 4 * i + k] = 1.0
    return np.concatenate([col.reshape(64, 32), row.reshape(64, 32)], axis=0)


def upward_packet(probes_t, basis_t, moves_t):
    leaves = [
        dot_t(probes_t[:, k * LEAF : (k + 1) * LEAF], basis_t[:, k * LEAF : (k + 1) * LEAF])
        for k in range(4)
    ]
    leaf = jnp.concatenate(leaves, axis=1).astype(BF16)
    mids = [
        dot_t(leaf[:, j * 128 : (j + 1) * 128], moves_t[:, j * 128 : (j + 1) * 128])
        for j in range(2)
    ]
    mid = jnp.concatenate(mids, axis=1).astype(BF16)
    top = dot_t(mid, moves_t[:, 256:384]).astype(BF16)
    halves = jnp.concatenate([top[:32], top[32:]], axis=1)
    halves = jnp.concatenate([halves, halves], axis=0)
    return jnp.concatenate([leaf, mid, halves], axis=1)


def matern(square):
    square = jnp.maximum(square, 1e-30)
    dist = square * lax.rsqrt(square)
    return (1.0 + RATE * dist) * jnp.exp2(dist * (-RATE2))


def split_dot(a, b):
    high = a.astype(BF16)
    low = (a - high.astype(F32)).astype(BF16)
    both = dot_n(jnp.concatenate([high, low], axis=0), b)
    return both[: a.shape[0]] + both[a.shape[0] :]


def features(sel, geo):
    flat = geo.astype(F32)
    squares = flat * flat
    norm = squares[0:4] + squares[4:8] + squares[8:12]
    high = norm.astype(BF16).astype(F32)
    rest = norm - high
    middle = rest.astype(BF16).astype(F32)
    low = rest - middle
    stack = jnp.concatenate([flat, high, middle, low, jnp.ones_like(norm)], axis=0)
    return dot_n(sel, stack.astype(BF16)).astype(BF16)


def prepare_kernel(
    near_list, near_count, far_list, far_count, points, skeleton,
    geo, near_pair, near_prev, near_last, far_prev, far_last, far_pair, far_side,
):
    pts = points[...].astype(F32)
    skel = skeleton[...].astype(F32)
    rows = []
    for i in range(3):
        for k in range(4):
            tail = skel[i : i + 1, k * 128 : min(k * 128 + 128, 448)]
            if k == 3:
                tail = jnp.concatenate([tail, jnp.zeros((1, 64), F32)], axis=1)
            rows.append(jnp.concatenate([pts[i : i + 1, k * LEAF : (k + 1) * LEAF], tail], axis=1))
    rows.append(jnp.zeros((4, GEO), F32))
    geo[...] = jnp.concatenate(rows, axis=0).astype(BF16)

    @pl.loop(0, FAR_MOST)
    def _(i):
        far_last[i] = 0
        far_prev[i] = 0
        for j in range(2):
            far_pair[j, i] = 0
            far_side[2 * j, i] = 0.0
            far_side[2 * j + 1, i] = 0.0

    @pl.loop(0, NEAR_MOST)
    def _(i):
        near_last[i] = 0
        near_prev[i] = 0
        for j in range(2):
            near_pair[j, i] = 0

    @pl.loop(0, near_count[0, 0] // 8)
    def _(g):
        for u in range(8):
            s = g * 8 + u
            a = near_list[0, s]
            near_pair[0, s] = a
            near_pair[1, s] = near_list[1, s]
            near_prev[s] = near_last[a]
            near_last[a] = s + 1

    @pl.loop(0, far_count[0, 0] // 8)
    def _(g):
        for u in range(8):
            s = g * 8 + u
            a = far_list[0, s]
            far_prev[s] = far_last[a]
            far_last[a] = s + 1
            for side in range(2):
                cluster = far_list[side, s]
                device = cluster // 7
                local = cluster - device * 7
                odd = (local % 2).astype(F32)
                far_pair[side, s] = device * 4 + local // 2
                far_side[2 * side, s] = 1.0 - odd
                far_side[2 * side + 1, s] = odd


def prepare(near_list, near_count, far_list, far_count, points, skeleton):
    vmem = pl.BlockSpec(memory_space=pltpu.VMEM)
    smem = pl.BlockSpec(memory_space=pltpu.SMEM)
    ints = lambda *shape: jax.ShapeDtypeStruct(shape, jnp.int32)
    return pl.pallas_call(
        prepare_kernel,
        out_shape=(
            jax.ShapeDtypeStruct((16, GEO), BF16),
            ints(2, NEAR_MOST), ints(NEAR_MOST), ints(NEAR_MOST), ints(FAR_MOST), ints(FAR_MOST), ints(2, FAR_MOST),
            jax.ShapeDtypeStruct((4, FAR_MOST), F32),
        ),
        in_specs=[smem, smem, smem, smem, vmem, vmem],
        out_specs=(vmem,) + (smem,) * 7,
        name="prepare",
    )(near_list, near_count, far_list, far_count, points, skeleton)


ORDER = (
    "g0", "b0", "a0", "up", "gz", "q0", "a10", "gy1", "by1", "q10", "gy2", "qz1", "gy3", "by2", "q13", "gy4",
    "qz2", "az1", "q11", "by3", "bz0", "gr", "F0", "q20", "q12", "a11", "F1", "bz1", "q21", "N2", "N7", "q23",
    "N1", "az2", "q22", "by4", "q30", "a13", "K2", "N0", "N3", "K0", "q33", "K3", "q31", "N4", "q32", "q40",
    "bz3", "a12", "a21", "K1", "q43", "N5", "q42", "a23", "bz2", "q41", "N6", "bz4", "a20", "a22", "U", "M0",
    "a31", "M1", "a33", "M2", "a30", "M3", "a32", "fs", "a43", "a41", "be", "fp", "a42", "a40", "nm", "rs", "end",
)


def main_kernel(
    order,
    near_pair, near_prev, near_last, far_prev, far_last, far_pair, far_side,
    sel, probes_t, basis_t, moves_t, geo,
    out,
    all_p, all_q, col_geo, row_geo, col_leaf, row_leaf, col_skel, row_skel,
    near_k, far_k, near_c, far_c, near_out, far_out,
    near_sib, far_sib, near_sum, far_sum, near_in, far_in,
    send, recv_a, recv_b, recv_q, geo_send, geo_recv, row_sems, ring_send, ring_recv, sems, sib_sems,
):
    r = lax.axis_index("row")
    c = lax.axis_index("col")
    zh = r // N_Y
    y = r % N_Y
    core = c % 2
    chip = c // 2
    sibling = chip * 2 + 1 - core

    def slot(dz, dy):
        return ((zh + dz) % N_ZH) * N_Y + (y + dy) % N_Y

    up, down, across = slot(1, 0), slot(3, 0), slot(2, 0)
    right, left = slot(0, 1), slot(0, -1)
    me = slot(0, 0)

    barrier = pltpu.get_barrier_semaphore()
    for row in (up, down, across, right, left):
        pl.semaphore_signal(barrier, inc=1, device_id=(row, c), device_id_type=MESH)

    @pl.loop(1, N_COL)
    def _(d):
        pl.semaphore_signal(
            barrier, inc=1, device_id=(r, (c + d) % N_COL), device_id_type=MESH
        )

    col_geo[y, zh] = geo[...]
    row_geo[c] = geo[...]
    for k in range(4):
        all_p[me * 4 + k] = probes_t[:, k * LEAF : (k + 1) * LEAF]
    pl.semaphore_wait(barrier, 5 + N_COL - 1)

    sends = []
    unsent = []

    def send_later(first, last, copy_of):
        def waits():
            @pl.loop(first, last)
            def _(d):
                copy_of(d).wait_send()

        unsent.append(waits)

    def copy(src, dst, sem, row):
        one = pltpu.make_async_remote_copy(
            src_ref=src, dst_ref=dst, send_sem=send.at[len(sends)], recv_sem=sem,
            device_id=(row, c), device_id_type=MESH,
        )
        one.start()
        sends.append(one)

    def arrived(dst, sem):
        pltpu.make_async_remote_copy(
            src_ref=dst, dst_ref=dst, send_sem=send.at[0], recv_sem=sem,
            device_id=(right, c), device_id_type=MESH,
        ).wait_recv()

    def mover(buf, sems, pitch, first, parts):
        def block(s, h=None):
            at = first + (0 if h != 1 else parts[0])
            return buf.at[pl.ds(s * pitch + at, sum(parts) if h is None else parts[h])]

        def push(s, row, h=None):
            copy(block(s, h), block(s, h), sems.at[s, h or 0], row)

        def wait(s, h=None):
            arrived(block(s, h), sems.at[s, h or 0])

        return push, wait

    movers = {
        "a": mover(all_p, recv_a, 4, 0, (1, 1)),
        "b": mover(all_p, recv_b, 4, 2, (1, 1)),
        "q": mover(all_q, recv_q, 8, 0, (4, 3)),
    }

    def ring(name, dz, k):
        push, wait = movers[name]
        if k == 4:
            wait(slot(dz, 4), 0)
            wait(slot(dz, 4), 1)
            return
        wait(slot(dz, -k))
        push(slot(dz, -k), right, 0 if k == 3 else None)
        wait(slot(dz, k))
        push(slot(dz, k), left, 1 if k == 3 else None)

    def turn(name, dy):
        push, wait = movers[name]
        wait(slot(3, dy))
        push(slot(3, dy), up, 0)
        wait(slot(1, dy))
        push(slot(1, dy), down, 1)

    def geo_z(d):
        return pltpu.make_async_remote_copy(
            src_ref=geo, dst_ref=col_geo.at[y, zh],
            send_sem=geo_send.at[d], recv_sem=geo_recv.at[d],
            device_id=(slot(d, 0), c), device_id_type=MESH,
        )

    def geo_y(k, way):
        place = (y - k) % N_Y if way == 0 else (y + k) % N_Y
        return pltpu.make_async_remote_copy(
            src_ref=col_geo.at[place], dst_ref=col_geo.at[place],
            send_sem=ring_send.at[way, k], recv_sem=ring_recv.at[way, k],
            device_id=(right if way == 0 else left, c), device_id_type=MESH,
        )

    def geo_y_wait(k, way):
        place = (y - k - 1) % N_Y if way == 0 else (y + k + 1) % N_Y
        arrived(col_geo.at[place], ring_recv.at[way, k])

    def geo_row(d):
        return pltpu.make_async_remote_copy(
            src_ref=geo, dst_ref=row_geo.at[c],
            send_sem=row_sems.at[0, d], recv_sem=row_sems.at[1, d],
            device_id=(r, (c + d) % N_COL), device_id_type=MESH,
        )

    def sib_copy(near, d):
        src, dst, at = (near_out, near_sib, 0) if near else (far_out, far_sib, 2)
        return pltpu.make_async_remote_copy(
            src_ref=src.at[d], dst_ref=dst.at[d],
            send_sem=sib_sems.at[at, d], recv_sem=sib_sems.at[at + 1, d],
            device_id=(r, sibling), device_id_type=MESH,
        )

    def chip_copy(near, d):
        src, dst, at = (near_sum, near_in, 0) if near else (far_sum, far_in, 2)
        return pltpu.make_async_remote_copy(
            src_ref=src.at[d], dst_ref=dst.at[d],
            send_sem=sems.at[at, d], recv_sem=sems.at[at + 1, d],
            device_id=(r, ((chip + d) % 8) * 2 + core), device_id_type=MESH,
        )

    def near_leaf(owner, k):
        return near_c[near_last[owner * 4 + k]]

    def far_whole(owner):
        parts = [far_c[far_last[owner * 7 + j]] for j in range(7)] + [jnp.zeros((64, 64), F32)]
        return jnp.concatenate(parts, axis=1)

    def event(e):
        if e == "g0":
            for d in (1, 2, 3):
                geo_z(d).start()

            @pl.loop(1, N_COL)
            def _(d):
                geo_row(d).start()

            send_later(1, 4, geo_z)
            send_later(1, N_COL, geo_row)

        elif e == "up":
            packet = upward_packet(probes_t[...], basis_t[...], moves_t[...])
            for j in range(7):
                rows = slice((j % 2) * 32, (j % 2) * 32 + 32)
                all_q[me * 8 + j] = packet[rows, (j // 2) * 128 : (j // 2) * 128 + 128]
        elif e in ("a0", "b0", "q0"):
            for row in (right, left, up, down) if e == "b0" else (up, down, right, left):
                movers[e[0]][0](me, row)
        elif e == "gz":
            for d in (1, 2, 3):
                arrived(col_geo.at[y, (zh - d) % N_ZH], geo_recv.at[d])
            geo_y(0, 0).start()
            geo_y(0, 1).start()
            send_later(0, 4, lambda k: geo_y(k, 0))
            send_later(0, 3, lambda k: geo_y(k, 1))
        elif e in ("gy1", "gy2", "gy3", "gy4"):
            k = int(e[2])
            geo_y_wait(k - 1, 0)
            if k < 4:
                geo_y(k, 0).start()
                geo_y_wait(k - 1, 1)
                if k < 3:
                    geo_y(k, 1).start()
        elif e in ("az1", "qz1"):
            turn(e[0], 0)
            for dz in (3, 1):
                movers[e[0]][0](slot(dz, 0), right)
                movers[e[0]][0](slot(dz, 0), left)
        elif e in ("az2", "qz2"):
            push, wait = movers[e[0]]
            wait(slot(2, 0), 0)
            wait(slot(2, 0), 1)
            push(slot(2, 0), right)
            push(slot(2, 0), left)
        elif e[0] in "aq":
            ring(e[0], int(e[2]), int(e[1]))
        elif e[:2] == "by":
            k = int(e[2])
            ring("b", 0, k)
            for dy in (-k, k) if k < 4 else (4,):
                movers["b"][0](slot(0, dy), up)
                movers["b"][0](slot(0, dy), down)
        elif e[:2] == "bz":
            k = int(e[2])
            for dy in (-k, k) if 0 < k < 4 else (k,):
                turn("b", dy)
        elif e == "be":
            for dy in (0, -1, 1, -2, 2, -3, 3, 4):
                movers["b"][1](slot(2, dy), 0)
                movers["b"][1](slot(2, dy), 1)
        elif e == "gr":

            @pl.loop(1, N_COL)
            def _(d):
                arrived(row_geo.at[(c + N_COL - d) % N_COL], row_sems.at[1, d])

        elif e[0] == "F":
            part = int(e[1])

            @pl.loop(part * 4, part * 4 + 4)
            def _(j):
                wide = jnp.concatenate([col_geo[j, k] for k in range(N_ZH)], axis=1)
                feat = features(sel[0:64], wide)
                for k in range(N_ZH):
                    store_features(col_leaf, col_skel, k * N_Y + j, feat[:, k * GEO : (k + 1) * GEO])

            @pl.loop(part * 2, part * 2 + 2)
            def _(j):
                wide = jnp.concatenate([row_geo[j * 4 + k] for k in range(4)], axis=1)
                feat = features(sel[64:128], wide)
                for k in range(4):
                    store_features(row_leaf, row_skel, j * 4 + k, feat[:, k * GEO : (k + 1) * GEO])

        elif e[0] == "N":
            for u in range(8):
                s = int(e[1]) * 8 + u
                square = dot_l(col_leaf[near_pair[1, s]], row_leaf[near_pair[0, s]])
                near_k[s] = matern(square).astype(BF16)
        elif e[0] == "K":

            @pl.loop(int(e[1]) * 2, int(e[1]) * 2 + 2)
            def _(g):
                for u in range(16):
                    s = g * 16 + u
                    ours = one_of(col_skel[far_pair[1, s]], far_side[2, s], far_side[3, s])
                    theirs = one_of(row_skel[far_pair[0, s]], far_side[0, s], far_side[1, s])
                    kern = matern(dot_l(ours, theirs))
                    far_k[s, 0:64] = (kern * far_side[2, s]).astype(BF16)
                    far_k[s, 64:128] = (kern * far_side[3, s]).astype(BF16)

        elif e == "U":
            far_c[0] = jnp.zeros((64, 64), F32)

            @pl.loop(0, N_ROW // 4)
            def _(g):
                for u in range(4):
                    d = g * 4 + u
                    top = all_q[d * 8 + 6]
                    all_q[d * 8 + 7] = jnp.concatenate([top[:, 64:], top[:, :64]], axis=1)

        elif e[0] == "M":

            @pl.loop(int(e[1]) * 2, int(e[1]) * 2 + 2)
            def _(g):
                for u in range(16):
                    s = g * 16 + u
                    at = far_pair[1, s] * 2
                    pair = jnp.concatenate([all_q[at], all_q[at + 1]], axis=0)
                    far_c[s + 1] = far_c[far_prev[s]] + dot_n(pair, far_k[s])

        elif e == "fs":

            @pl.loop(0, 8)
            def _(i):
                d = 7 - i
                far_out[d] = far_whole(((chip + d) % 8) * 2 + 1 - core).astype(BF16)
                sib_copy(False, d).start()

            send_later(0, 8, functools.partial(sib_copy, False))

        elif e == "fp":

            @pl.loop(0, 7)
            def _(i):
                d = 7 - i
                sib_copy(False, d).wait_recv()
                own = far_whole(((chip + d) % 8) * 2 + core)
                far_sum[d] = (own + far_sib[d].astype(F32)).astype(BF16)
                chip_copy(False, d).start()

            send_later(1, 8, functools.partial(chip_copy, False))

        elif e == "nm":
            near_c[0] = jnp.zeros((SAMPLES, LEAF), F32)

            @pl.loop(0, NEAR_MOST // 4)
            def _(g):
                for u in range(4):
                    s = g * 4 + u
                    near_c[s + 1] = near_c[near_prev[s]] + dot_n(all_p[near_pair[1, s]], near_k[s])

        elif e == "rs":

            @pl.loop(0, 8)
            def _(i):
                d = 7 - i
                owner = ((chip + d) % 8) * 2 + 1 - core
                for k in range(4):
                    near_out[d, :, k * LEAF : (k + 1) * LEAF] = near_leaf(owner, k).astype(BF16)
                sib_copy(True, d).start()

            send_later(0, 8, functools.partial(sib_copy, True))

            @pl.loop(0, 7)
            def _(i):
                d = 7 - i
                sib_copy(True, d).wait_recv()
                owner = ((chip + d) % 8) * 2 + core
                for k in range(4):
                    lanes = slice(k * LEAF, (k + 1) * LEAF)
                    theirs = near_sib[d, :, lanes].astype(F32)
                    near_sum[d, :, lanes] = (near_leaf(owner, k) + theirs).astype(BF16)
                chip_copy(True, d).start()

            send_later(1, 8, functools.partial(chip_copy, True))

        elif e == "end":
            sib_copy(False, 0).wait_recv()
            far_total = far_whole(c) + far_sib[0].astype(F32)
            for d in range(1, 8):
                chip_copy(False, d).wait_recv()
                far_total = far_total + far_in[d].astype(F32)
            top = far_total[:, 384:448]
            middle = far_total[:, 256:384] + split_dot(top, moves_t[:, 256:384])
            sib_copy(True, 0).wait_recv()
            sums = []
            for k in range(4):
                leaf = far_total[:, k * 64 : (k + 1) * 64] + split_dot(
                    middle[:, (k // 2) * 64 : (k // 2) * 64 + 64], moves_t[:, k * 64 : (k + 1) * 64]
                )
                lanes = slice(k * LEAF, (k + 1) * LEAF)
                sums.append(
                    near_leaf(c, k) + near_sib[0, :, lanes].astype(F32) + split_dot(leaf, basis_t[:, lanes])
                )
            for d in range(1, 8):
                chip_copy(True, d).wait_recv()
            for k in range(4):
                lanes = slice(k * LEAF, (k + 1) * LEAF)
                total = sums[k]
                for d in range(1, 8):
                    total = total + near_in[d, :, lanes].astype(F32)
                out[:, lanes] = total.astype(BF16)

    def store_features(leaf, skel, d, feat):
        leaf[pl.ds(d * 4, 4)] = feat[:, 0:256].reshape(4, 16, 256)
        skel[pl.ds(d * 4, 4)] = feat[:, 256:384].reshape(4, 16, 128)

    def one_of(pair, first, second):
        pair = pair.astype(F32)
        return (pair[:, :64] * first + pair[:, 64:] * second).astype(BF16)

    for e in order:
        event(e)

    for one in unsent:
        one()
    for one in sends:
        one.wait_send()


def run(chains, sel, probes_t, basis_t, moves_t, geo, order=ORDER):
    vmem = pl.BlockSpec(memory_space=pltpu.VMEM)
    smem = pl.BlockSpec(memory_space=pltpu.SMEM)
    dma = pltpu.SemaphoreType.DMA
    return pl.pallas_call(
        functools.partial(main_kernel, order),
        out_shape=jax.ShapeDtypeStruct((64, 1024), BF16),
        in_specs=[smem] * 7 + [vmem] * 5,
        out_specs=vmem,
        scratch_shapes=[
            pltpu.VMEM((4 * N_ROW, 64, LEAF), BF16),
            pltpu.VMEM((8 * N_ROW, 32, 128), BF16),
            pltpu.VMEM((N_Y, N_ZH, 16, GEO), BF16),
            pltpu.VMEM((N_COL, 16, GEO), BF16),
            pltpu.VMEM((4 * N_ROW, 16, LEAF), BF16),
            pltpu.VMEM((4 * N_COL, 16, LEAF), BF16),
            pltpu.VMEM((4 * N_ROW, 16, 128), BF16),
            pltpu.VMEM((4 * N_COL, 16, 128), BF16),
            pltpu.VMEM((NEAR_MOST, LEAF, LEAF), BF16),
            pltpu.VMEM((FAR_MOST, 2 * RANK, RANK), BF16),
            pltpu.VMEM((NEAR_MOST + 1, SAMPLES, LEAF), F32),
            pltpu.VMEM((FAR_MOST + 1, SAMPLES, RANK), F32),
            pltpu.VMEM((8, 64, 1024), BF16),
            pltpu.VMEM((8, 64, 512), BF16),
            pltpu.VMEM((8, 64, 1024), BF16),
            pltpu.VMEM((8, 64, 512), BF16),
            pltpu.VMEM((8, 64, 1024), BF16),
            pltpu.VMEM((8, 64, 512), BF16),
            pltpu.VMEM((8, 64, 1024), BF16),
            pltpu.VMEM((8, 64, 512), BF16),
            dma((120,)),
            dma((N_ROW, 2)),
            dma((N_ROW, 2)),
            dma((N_ROW, 2)),
            dma((4,)),
            dma((4,)),
            dma((2, N_COL)),
            dma((2, 4)),
            dma((2, 4)),
            dma((4, 8)),
            dma((4, 8)),
        ],
        compiler_params=pltpu.CompilerParams(
            collective_id=0, has_side_effects=True, vmem_limit_bytes=56 << 20
        ),
        name="sample",
    )(*chains, sel, probes_t, basis_t, moves_t, geo)


def local(
    probes, points, skeleton, leaf_basis, transfer, near_list, near_count, far_list, far_count
):
    probes_t, basis_t, moves_t = probes.T, leaf_basis.T, transfer.T
    sel = jnp.asarray(selections(), BF16)
    near_pairs, far_pairs = near_list[0, 0], far_list[0, 0]
    geo, *chains = prepare(near_pairs, near_count, far_pairs, far_count, points, skeleton)
    return run(chains, sel, probes_t, basis_t, moves_t, geo).T


def solution(mesh):
    placed = (
        P(("row", "col"), None),
        P(None, ("row", "col")),
        P(None, ("row", "col")),
        P(("row", "col"), None),
        P(("row", "col"), None),
        P("row", "col", None, None),
        P("row", "col"),
        P("row", "col", None, None),
        P("row", "col"),
    )
    return jax.shard_map(
        local, mesh=mesh, in_specs=placed, out_specs=P(("row", "col"), None), check_vma=False
    )
```

```python
import functools
import math

import jax
import jax.numpy as jnp
import numpy as np
from jax import lax
from jax.experimental import pallas as pl
from jax.experimental.pallas import tpu as pltpu
from jax.sharding import PartitionSpec as P

LEAF = 256
RANK = 64
SAMPLES = 64
N_ROW = 32
N_COL = 16
N_Y = 8
N_ZH = 4
NEAR_MOST = 64
FAR_MOST = 128
GEO = 384
MESH = pl.DeviceIdType.MESH
F32 = jnp.float32
BF16 = jnp.bfloat16
RATE = math.sqrt(3.0) / 0.15
RATE2 = RATE * math.log2(math.e)


def dot_t(a, b):
    return lax.dot_general(a, b, (((1,), (1,)), ((), ())), preferred_element_type=F32)


def dot_l(a, b):
    return lax.dot_general(a, b, (((0,), (0,)), ((), ())), preferred_element_type=F32)


def dot_n(a, b):
    return jnp.dot(a, b, preferred_element_type=F32)


def selections():
    col = np.zeros((4, 16, 32), np.float32)
    row = np.zeros((4, 16, 32), np.float32)
    for k in range(4):
        for i in range(3):
            col[k, i, i * 4 + k] = -2.0
            row[k, i, i * 4 + k] = 1.0
            col[k, 3 + i, 16 + 4 * i + k] = 1.0
            row[k, 3 + i, 28] = 1.0
            col[k, 6 + i, 28] = 1.0
            row[k, 6 + i, 16 + 4 * i + k] = 1.0
    return np.concatenate([col.reshape(64, 32), row.reshape(64, 32)], axis=0)


def upward_packet(probes_t, basis_t, moves_t):
    leaves = [
        dot_t(probes_t[:, k * LEAF : (k + 1) * LEAF], basis_t[:, k * LEAF : (k + 1) * LEAF])
        for k in range(4)
    ]
    leaf = jnp.concatenate(leaves, axis=1).astype(BF16)
    mids = [
        dot_t(leaf[:, j * 128 : (j + 1) * 128], moves_t[:, j * 128 : (j + 1) * 128])
        for j in range(2)
    ]
    mid = jnp.concatenate(mids, axis=1).astype(BF16)
    top = dot_t(mid, moves_t[:, 256:384]).astype(BF16)
    halves = jnp.concatenate([top[:32], top[32:]], axis=1)
    halves = jnp.concatenate([halves, halves], axis=0)
    return jnp.concatenate([leaf, mid, halves], axis=1)


def matern(square):
    square = jnp.maximum(square, 1e-30)
    dist = square * lax.rsqrt(square)
    return (1.0 + RATE * dist) * jnp.exp2(dist * (-RATE2))


def split_dot(a, b):
    high = a.astype(BF16)
    low = (a - high.astype(F32)).astype(BF16)
    both = dot_n(jnp.concatenate([high, low], axis=0), b)
    return both[: a.shape[0]] + both[a.shape[0] :]


def features(sel, geo):
    flat = geo.astype(F32)
    squares = flat * flat
    norm = squares[0:4] + squares[4:8] + squares[8:12]
    high = norm.astype(BF16).astype(F32)
    rest = norm - high
    middle = rest.astype(BF16).astype(F32)
    low = rest - middle
    stack = jnp.concatenate([flat, high, middle, low, jnp.ones_like(norm)], axis=0)
    return dot_n(sel, stack.astype(BF16)).astype(BF16)


def packed(points, skeleton):
    pts = points.astype(F32)
    skel = skeleton.astype(F32)
    rows = []
    for i in range(3):
        for k in range(4):
            tail = skel[i : i + 1, k * 128 : min(k * 128 + 128, 448)]
            if k == 3:
                tail = jnp.concatenate([tail, jnp.zeros((1, 64), F32)], axis=1)
            rows.append(jnp.concatenate([pts[i : i + 1, k * LEAF : (k + 1) * LEAF], tail], axis=1))
    rows.append(jnp.zeros((4, GEO), F32))
    return jnp.concatenate(rows, axis=0).astype(BF16)


def chain(targets, live):
    across = jnp.broadcast_to(targets, (128, 128))
    down = across.T
    row = lax.broadcasted_iota(jnp.int32, (128, 128), 0)
    lane = lax.broadcasted_iota(jnp.int32, (128, 128), 1)
    prev = jnp.where((across == down) & (row < lane), row + 1, 0)
    last = jnp.where((down == lane) & (row < live), row + 1, 0)
    return jnp.max(prev, axis=0, keepdims=True), jnp.max(last, axis=0, keepdims=True)


def slot_tables(near_list, near_live, far_list, far_live):
    near = jnp.concatenate([near_list, jnp.zeros((2, 64), jnp.int32)], axis=1)
    target = jnp.clip(near[0:1], 0, 4 * N_COL - 1)
    source = jnp.clip(near[1:2], 0, 4 * N_ROW - 1)
    far_target = jnp.clip(far_list[0:1], 0, 7 * N_COL - 1)
    far_source = jnp.clip(far_list[1:2], 0, 7 * N_ROW - 1)
    far = jnp.concatenate([far_target, far_source], axis=0)
    device = (far * 9363) >> 16
    local = far - device * 7
    half = local >> 1
    odd = (local - half * 2).astype(F32)
    place = device * 4 + half
    index = jnp.concatenate(
        [target, source, *chain(target, near_live), place, *chain(far_target, far_live)], axis=0
    )
    weights = jnp.concatenate([1.0 - odd[0:1], odd[0:1], 1.0 - odd[1:2], odd[1:2]], axis=0)
    return index, jnp.concatenate([weights, jnp.zeros((4, 128), F32)], axis=0)


ORDER = (
    "g0", "a0", "up", "q0", "gz", "b0", "a10", "q10", "gy1", "qz1", "by1", "gy2", "q13", "gr", "qz2", "bz0", "T",
    "by2", "gy3", "q11", "q20", "q12", "az1", "gy4", "W", "F0", "by3", "F1", "q23", "q21", "K1", "q22", "N0",
    "K0", "az2", "N4", "q30", "N5", "a11", "bz1", "N1", "q33", "q31", "bz2", "q32", "bz3", "a12", "a13", "by4",
    "K3", "K2", "a20", "a21", "q43", "N6", "q42", "q40", "q41", "U", "M0", "a22", "M1", "a23", "M2", "M3", "a30",
    "fs", "a31", "a32", "N3", "a33", "bz4", "xf", "N7", "N2", "a41", "a40", "a43", "a42", "na", "sa", "be", "nb",
    "xa", "sb", "cf", "xb", "ca", "ef", "ea", "eb",
)


def main_kernel(
    order,
    near_count, far_count, near_list, far_list, sel, points, skeleton, probes_t, basis_t, moves_t,
    out,
    geo, index_v, index, weight_v, weight, table_sems,
    all_a, all_b, all_q, col_geo, row_geo, col_leaf, row_leaf, col_skel, row_skel,
    near_k, far_k, near_ca, near_cb, far_c, near_out, far_out,
    near_sib, far_sib, near_sum, far_sum, near_in, far_in, far_part,
    send, recv_a, recv_b, recv_q, geo_send, geo_recv, row_sems, ring_send, ring_recv, sems, sib_sems,
):
    r = lax.axis_index("row")
    c = lax.axis_index("col")
    zh = lax.div(r, N_Y)
    y = lax.rem(r, N_Y)
    core = lax.rem(c, 2)
    chip = lax.div(c, 2)
    sibling = chip * 2 + 1 - core
    z_lo = lax.div(chip, 4)
    x = lax.rem(chip, 4)

    def slot(dz, dy):
        return lax.rem(zh + dz, N_ZH) * N_Y + lax.rem(y + dy % N_Y, N_Y)

    up, down, across = slot(1, 0), slot(3, 0), slot(2, 0)
    right, left = slot(0, 1), slot(0, -1)
    me = slot(0, 0)

    barrier = pltpu.get_barrier_semaphore()
    for row in (up, down, across, right, left):
        pl.semaphore_signal(barrier, inc=1, device_id=(row, c), device_id_type=MESH)

    @pl.loop(1, N_COL)
    def _(d):
        pl.semaphore_signal(
            barrier, inc=1, device_id=(r, (c + d) % N_COL), device_id_type=MESH
        )

    geo[...] = packed(points[...], skeleton[...])
    col_geo[y, zh] = geo[...]
    row_geo[c] = geo[...]
    for k in range(4):
        all_a[me * 4 + k] = probes_t[0:32, k * LEAF : (k + 1) * LEAF]
        all_b[me * 4 + k] = probes_t[32:64, k * LEAF : (k + 1) * LEAF]
    pl.semaphore_wait(barrier, 5 + N_COL - 1)

    sends = []
    unsent = []

    def send_later(first, last, copy_of):
        def waits():
            @pl.loop(first, last)
            def _(d):
                copy_of(d).wait_send()

        unsent.append(waits)

    def copy(src, dst, sem, row):
        one = pltpu.make_async_remote_copy(
            src_ref=src, dst_ref=dst, send_sem=send.at[len(sends)], recv_sem=sem,
            device_id=(row, c), device_id_type=MESH,
        )
        one.start()
        sends.append(one)

    def arrived(dst, sem):
        pltpu.make_async_remote_copy(
            src_ref=dst, dst_ref=dst, send_sem=send.at[0], recv_sem=sem,
            device_id=(right, c), device_id_type=MESH,
        ).wait_recv()

    def mover(buf, sems, pitch, parts):
        def block(s, h=None):
            at = 0 if h != 1 else parts[0]
            return buf.at[pl.ds(s * pitch + at, sum(parts) if h is None else parts[h])]

        def push(s, row, h=None):
            copy(block(s, h), block(s, h), sems.at[s, h or 0], row)

        def wait(s, h=None):
            arrived(block(s, h), sems.at[s, h or 0])

        return push, wait

    movers = {
        "a": mover(all_a, recv_a, 4, (2, 2)),
        "b": mover(all_b, recv_b, 4, (2, 2)),
        "q": mover(all_q, recv_q, 8, (4, 3)),
    }

    def ring(name, dz, k):
        push, wait = movers[name]
        if k == 4:
            wait(slot(dz, 4), 0)
            wait(slot(dz, 4), 1)
            return
        wait(slot(dz, -k))
        push(slot(dz, -k), right, 0 if k == 3 else None)
        wait(slot(dz, k))
        push(slot(dz, k), left, 1 if k == 3 else None)

    def turn(name, dy):
        push, wait = movers[name]
        wait(slot(3, dy))
        push(slot(3, dy), up, 0)
        wait(slot(1, dy))
        push(slot(1, dy), down, 1)

    def geo_z(d):
        return pltpu.make_async_remote_copy(
            src_ref=geo, dst_ref=col_geo.at[y, zh],
            send_sem=geo_send.at[d], recv_sem=geo_recv.at[d],
            device_id=(slot(d, 0), c), device_id_type=MESH,
        )

    def geo_y(k, way):
        place = (y - k) % N_Y if way == 0 else (y + k) % N_Y
        return pltpu.make_async_remote_copy(
            src_ref=col_geo.at[place], dst_ref=col_geo.at[place],
            send_sem=ring_send.at[way, k], recv_sem=ring_recv.at[way, k],
            device_id=(right if way == 0 else left, c), device_id_type=MESH,
        )

    def geo_y_wait(k, way):
        place = (y - k - 1) % N_Y if way == 0 else (y + k + 1) % N_Y
        arrived(col_geo.at[place], ring_recv.at[way, k])

    def geo_row(d):
        return pltpu.make_async_remote_copy(
            src_ref=geo, dst_ref=row_geo.at[c],
            send_sem=row_sems.at[0, d], recv_sem=row_sems.at[1, d],
            device_id=(r, (c + d) % N_COL), device_id_type=MESH,
        )

    outs = (near_out.at[0], near_out.at[1], far_out)
    sibs = (near_sib.at[0], near_sib.at[1], far_sib)
    whole = (near_sum.at[0], near_sum.at[1], far_sum)
    comes = (near_in.at[0], near_in.at[1], far_in)

    def sib_copy(what, d):
        return pltpu.make_async_remote_copy(
            src_ref=outs[what].at[d], dst_ref=sibs[what].at[d],
            send_sem=sib_sems.at[2 * what, d], recv_sem=sib_sems.at[2 * what + 1, d],
            device_id=(r, sibling), device_id_type=MESH,
        )

    def chip_at(d):
        return lax.rem(z_lo + lax.div(d, 4), 2) * 4 + lax.rem(x + lax.rem(d, 4), 4)

    def chip_copy(what, d, by_x=False):
        to = chip_at(lax.rem(d, 4) if by_x else d)
        return pltpu.make_async_remote_copy(
            src_ref=whole[what].at[d], dst_ref=comes[what].at[d],
            send_sem=sems.at[2 * what, d], recv_sem=sems.at[2 * what + 1, d],
            device_id=(r, to * 2 + core), device_id_type=MESH,
        )

    def core_sum(what, d):
        sib_copy(what, d).wait_recv()
        owner = chip_at(d) * 2 + core
        if what == 2:
            far_sum[d] = (far_whole(owner) + far_sib[d].astype(F32)).astype(BF16)
            return
        for k in range(4):
            lanes = slice(k * LEAF, (k + 1) * LEAF)
            theirs = near_sib[what, d, :, lanes].astype(F32)
            near_sum[what, d, :, lanes] = (near_leaf(what, owner, k) + theirs).astype(BF16)

    def spread(what):
        @pl.loop(0, 7)
        def _(i):
            core_sum(what, 7 - i)
            chip_copy(what, 7 - i).start()

        send_later(1, 8, functools.partial(chip_copy, what))

    def spread_x(what):
        for first in (5, 1):

            @pl.loop(0, 3)
            def _(i):
                d = first + 2 - i
                core_sum(what, d)
                chip_copy(what, d, True).start()

            send_later(first, first + 3, functools.partial(chip_copy, what, by_x=True))

        core_sum(what, 4)

    def cross(what):
        total = whole[what][4].astype(F32)
        for d in (5, 6, 7):
            chip_copy(what, d, True).wait_recv()
            total = total + comes[what][d].astype(F32)
        whole[what][4] = total.astype(BF16)
        chip_copy(what, 4).start()
        send_later(4, 5, functools.partial(chip_copy, what))

    def near_leaf(h, owner, k):
        return (near_ca, near_cb)[h][index[3, owner * 4 + k]]

    def far_whole(owner):
        parts = [far_c[index[7, owner * 7 + j]] for j in range(7)] + [jnp.zeros((64, 64), F32)]
        return jnp.concatenate(parts, axis=1)

    tables = (
        pltpu.make_async_copy(index_v, index, table_sems.at[0]),
        pltpu.make_async_copy(weight_v, weight, table_sems.at[1]),
    )

    def event(e):
        if e == "g0":
            for d in (1, 2, 3):
                geo_z(d).start()

            @pl.loop(1, N_COL)
            def _(d):
                geo_row(d).start()

            send_later(1, 4, geo_z)
            send_later(1, N_COL, geo_row)

        elif e == "up":
            packet = upward_packet(probes_t[...], basis_t[...], moves_t[...])
            for j in range(7):
                rows = slice((j % 2) * 32, (j % 2) * 32 + 32)
                all_q[me * 8 + j] = packet[rows, (j // 2) * 128 : (j // 2) * 128 + 128]
        elif e in ("a0", "b0", "q0"):
            for row in (right, left, up, down) if e == "b0" else (up, down, right, left):
                movers[e[0]][0](me, row)
        elif e == "gz":
            for d in (1, 2, 3):
                arrived(col_geo.at[y, (zh - d) % N_ZH], geo_recv.at[d])
            geo_y(0, 0).start()
            geo_y(0, 1).start()
            send_later(0, 4, lambda k: geo_y(k, 0))
            send_later(0, 3, lambda k: geo_y(k, 1))
        elif e in ("gy1", "gy2", "gy3", "gy4"):
            k = int(e[2])
            geo_y_wait(k - 1, 0)
            if k < 4:
                geo_y(k, 0).start()
                geo_y_wait(k - 1, 1)
                if k < 3:
                    geo_y(k, 1).start()
        elif e in ("az1", "qz1"):
            turn(e[0], 0)
            for dz in (3, 1):
                movers[e[0]][0](slot(dz, 0), right)
                movers[e[0]][0](slot(dz, 0), left)
        elif e in ("az2", "qz2"):
            push, wait = movers[e[0]]
            wait(slot(2, 0), 0)
            wait(slot(2, 0), 1)
            push(slot(2, 0), right)
            push(slot(2, 0), left)
        elif e[0] in "aq":
            ring(e[0], int(e[2]), int(e[1]))
        elif e[:2] == "by":
            k = int(e[2])
            ring("b", 0, k)
            for dy in (-k, k) if k < 4 else (4,):
                movers["b"][0](slot(0, dy), up)
                movers["b"][0](slot(0, dy), down)
        elif e[:2] == "bz":
            k = int(e[2])
            for dy in (-k, k) if 0 < k < 4 else (k,):
                turn("b", dy)
        elif e == "be":
            for dy in (0, -1, 1, -2, 2, -3, 3, 4):
                movers["b"][1](slot(2, dy), 0)
                movers["b"][1](slot(2, dy), 1)
        elif e == "gr":

            @pl.loop(1, N_COL)
            def _(d):
                arrived(row_geo.at[(c + N_COL - d) % N_COL], row_sems.at[1, d])

        elif e[0] == "F":
            part = int(e[1])

            @pl.loop(part * 4, part * 4 + 4)
            def _(j):
                wide = jnp.concatenate([col_geo[j, k] for k in range(N_ZH)], axis=1)
                feat = features(sel[0:64], wide)
                for k in range(N_ZH):
                    store_features(col_leaf, col_skel, k * N_Y + j, feat[:, k * GEO : (k + 1) * GEO])

            @pl.loop(part * 2, part * 2 + 2)
            def _(j):
                wide = jnp.concatenate([row_geo[j * 4 + k] for k in range(4)], axis=1)
                feat = features(sel[64:128], wide)
                for k in range(4):
                    store_features(row_leaf, row_skel, j * 4 + k, feat[:, k * GEO : (k + 1) * GEO])

        elif e[0] == "N":
            for u in range(8):
                s = int(e[1]) * 8 + u
                square = dot_l(col_leaf[index[1, s]], row_leaf[index[0, s]])
                near_k[s] = matern(square).astype(BF16)
        elif e[0] == "K":

            @pl.loop(int(e[1]) * 2, int(e[1]) * 2 + 2)
            def _(g):
                for u in range(16):
                    s = g * 16 + u
                    ours = one_of(col_skel[index[5, s]], weight[2, s], weight[3, s])
                    theirs = one_of(row_skel[index[4, s]], weight[0, s], weight[1, s])
                    kern = matern(dot_l(ours, theirs))
                    far_k[s, 0:64] = (kern * weight[2, s]).astype(BF16)
                    far_k[s, 64:128] = (kern * weight[3, s]).astype(BF16)

        elif e == "U":
            far_c[0] = jnp.zeros((64, 64), F32)

            @pl.loop(0, N_ROW // 4)
            def _(g):
                for u in range(4):
                    d = g * 4 + u
                    top = all_q[d * 8 + 6]
                    all_q[d * 8 + 7] = jnp.concatenate([top[:, 64:], top[:, :64]], axis=1)

        elif e[0] == "M":

            @pl.loop(int(e[1]) * 2, int(e[1]) * 2 + 2)
            def _(g):
                for u in range(16):
                    s = g * 16 + u
                    at = index[5, s] * 2
                    pair = jnp.concatenate([all_q[at], all_q[at + 1]], axis=0)
                    far_c[s + 1] = far_c[index[6, s]] + dot_n(pair, far_k[s])

        elif e == "fs":

            @pl.loop(0, 8)
            def _(i):
                d = 7 - i
                far_out[d] = far_whole(chip_at(d) * 2 + 1 - core).astype(BF16)
                sib_copy(2, d).start()

            send_later(0, 8, functools.partial(sib_copy, 2))

        elif e in ("xa", "xf"):
            spread_x(0 if e == "xa" else 2)
        elif e in ("ca", "cf"):
            cross(0 if e == "ca" else 2)
        elif e == "xb":
            spread(1)
        elif e in ("na", "nb"):
            sums, samples = (near_ca, all_a) if e == "na" else (near_cb, all_b)
            sums[0] = jnp.zeros((32, LEAF), F32)

            @pl.loop(0, NEAR_MOST // 16)
            def _(g):
                for u in range(16):
                    s = g * 16 + u
                    sums[s + 1] = sums[index[2, s]] + dot_n(samples[index[1, s]], near_k[s])

        elif e in ("sa", "sb"):
            h = "ab".index(e[1])

            @pl.loop(0, 8)
            def _(i):
                d = 7 - i
                owner = chip_at(d) * 2 + 1 - core
                for k in range(4):
                    near_out[h, d, :, k * LEAF : (k + 1) * LEAF] = near_leaf(h, owner, k).astype(BF16)
                sib_copy(h, d).start()

            send_later(0, 8, functools.partial(sib_copy, h))
        elif e == "ef":
            sib_copy(2, 0).wait_recv()
            total = far_whole(c) + far_sib[0].astype(F32)
            for d in range(1, 5):
                chip_copy(2, d).wait_recv()
                total = total + far_in[d].astype(F32)
            middle = total[:, 256:384] + split_dot(total[:, 384:448], moves_t[:, 256:384])
            for k in range(4):
                leaf = total[:, k * 64 : (k + 1) * 64] + split_dot(
                    middle[:, (k // 2) * 64 : (k // 2) * 64 + 64], moves_t[:, k * 64 : (k + 1) * 64]
                )
                lanes = slice(k * LEAF, (k + 1) * LEAF)
                far_part[:, lanes] = split_dot(leaf, basis_t[:, lanes])
        elif e in ("ea", "eb"):
            h = "ab".index(e[1])
            rows = slice(32 * h, 32 * h + 32)
            sib_copy(h, 0).wait_recv()
            others = range(1, 5) if h == 0 else range(1, 8)
            for d in others:
                chip_copy(h, d).wait_recv()
            for k in range(4):
                lanes = slice(k * LEAF, (k + 1) * LEAF)
                total = near_leaf(h, c, k) + near_sib[h, 0, :, lanes].astype(F32) + far_part[rows, lanes]
                for d in others:
                    total = total + near_in[h, d, :, lanes].astype(F32)
                out[rows, lanes] = total.astype(BF16)
        elif e == "T":
            index_v[...], weight_v[...] = slot_tables(
                near_list[...], near_count[0, 0], far_list[...], far_count[0, 0]
            )
            for one in tables:
                one.start()
        elif e == "W":
            for one in tables:
                one.wait()
        else:
            raise ValueError(e)

    def store_features(leaf, skel, d, feat):
        leaf[pl.ds(d * 4, 4)] = feat[:, 0:256].reshape(4, 16, 256)
        skel[pl.ds(d * 4, 4)] = feat[:, 256:384].reshape(4, 16, 128)

    def one_of(pair, first, second):
        pair = pair.astype(F32)
        return (pair[:, :64] * first + pair[:, 64:] * second).astype(BF16)

    for e in order:
        event(e)

    for one in unsent:
        one()
    for one in sends:
        one.wait_send()


def run(near_count, far_count, near_list, far_list, sel, points, skeleton, probes_t, basis_t, moves_t):
    vmem = pl.BlockSpec(memory_space=pltpu.VMEM)
    smem = pl.BlockSpec(memory_space=pltpu.SMEM)
    dma = pltpu.SemaphoreType.DMA
    return pl.pallas_call(
        functools.partial(main_kernel, ORDER),
        out_shape=jax.ShapeDtypeStruct((64, 1024), BF16),
        in_specs=[smem] * 2 + [vmem] * 8,
        out_specs=vmem,
        scratch_shapes=[
            pltpu.VMEM((16, GEO), BF16),
            pltpu.VMEM((8, 128), jnp.int32),
            pltpu.SMEM((8, 128), jnp.int32),
            pltpu.VMEM((8, 128), F32),
            pltpu.SMEM((8, 128), F32),
            dma((2,)),
            pltpu.VMEM((4 * N_ROW, 32, LEAF), BF16),
            pltpu.VMEM((4 * N_ROW, 32, LEAF), BF16),
            pltpu.VMEM((8 * N_ROW, 32, 128), BF16),
            pltpu.VMEM((N_Y, N_ZH, 16, GEO), BF16),
            pltpu.VMEM((N_COL, 16, GEO), BF16),
            pltpu.VMEM((4 * N_ROW, 16, LEAF), BF16),
            pltpu.VMEM((4 * N_COL, 16, LEAF), BF16),
            pltpu.VMEM((4 * N_ROW, 16, 128), BF16),
            pltpu.VMEM((4 * N_COL, 16, 128), BF16),
            pltpu.VMEM((NEAR_MOST, LEAF, LEAF), BF16),
            pltpu.VMEM((FAR_MOST, 2 * RANK, RANK), BF16),
            pltpu.VMEM((NEAR_MOST + 1, 32, LEAF), F32),
            pltpu.VMEM((NEAR_MOST + 1, 32, LEAF), F32),
            pltpu.VMEM((FAR_MOST + 1, SAMPLES, RANK), F32),
            pltpu.VMEM((2, 8, 32, 1024), BF16),
            pltpu.VMEM((8, 64, 512), BF16),
            pltpu.VMEM((2, 8, 32, 1024), BF16),
            pltpu.VMEM((8, 64, 512), BF16),
            pltpu.VMEM((2, 8, 32, 1024), BF16),
            pltpu.VMEM((8, 64, 512), BF16),
            pltpu.VMEM((2, 8, 32, 1024), BF16),
            pltpu.VMEM((8, 64, 512), BF16),
            pltpu.VMEM((64, 1024), F32),
            dma((120,)),
            dma((N_ROW, 2)),
            dma((N_ROW, 2)),
            dma((N_ROW, 2)),
            dma((4,)),
            dma((4,)),
            dma((2, N_COL)),
            dma((2, 4)),
            dma((2, 4)),
            dma((6, 8)),
            dma((6, 8)),
        ],
        compiler_params=pltpu.CompilerParams(
            collective_id=0, has_side_effects=True, vmem_limit_bytes=56 << 20
        ),
        name="sample",
    )(near_count, far_count, near_list, far_list, sel, points, skeleton, probes_t, basis_t, moves_t)


def local(
    probes, points, skeleton, leaf_basis, transfer, near_list, near_count, far_list, far_count
):
    sel = jnp.asarray(selections(), BF16)
    return run(
        near_count, far_count, near_list[0, 0], far_list[0, 0],
        sel, points, skeleton, probes.T, leaf_basis.T, transfer.T,
    ).T


def solution(mesh):
    placed = (
        P(("row", "col"), None),
        P(None, ("row", "col")),
        P(None, ("row", "col")),
        P(("row", "col"), None),
        P(("row", "col"), None),
        P("row", "col", None, None),
        P("row", "col"),
        P("row", "col", None, None),
        P("row", "col"),
    )
    return jax.shard_map(
        local, mesh=mesh, in_specs=placed, out_specs=P(("row", "col"), None), check_vma=False
    )
```

```python
import functools
import math

import jax
import jax.numpy as jnp
import numpy as np
from jax import lax
from jax.experimental import pallas as pl
from jax.experimental.pallas import tpu as pltpu
from jax.sharding import PartitionSpec as P

LEAF = 256
RANK = 64
SAMPLES = 64
N_ROW = 32
N_COL = 16
N_Y = 8
N_ZH = 4
NEAR_MOST = 64
FAR_MOST = 128
GEO = 384
MESH = pl.DeviceIdType.MESH
F32 = jnp.float32
BF16 = jnp.bfloat16
RATE = math.sqrt(3.0) / 0.15
RATE2 = RATE * math.log2(math.e)


def dot_t(a, b):
    return lax.dot_general(a, b, (((1,), (1,)), ((), ())), preferred_element_type=F32)


def dot_l(a, b):
    return lax.dot_general(a, b, (((0,), (0,)), ((), ())), preferred_element_type=F32)


def dot_n(a, b):
    return jnp.dot(a, b, preferred_element_type=F32)


def selections():
    col = np.zeros((4, 16, 32), np.float32)
    row = np.zeros((4, 16, 32), np.float32)
    for k in range(4):
        for i in range(3):
            col[k, i, i * 4 + k] = -2.0
            row[k, i, i * 4 + k] = 1.0
            col[k, 3 + i, 16 + 4 * i + k] = 1.0
            row[k, 3 + i, 28] = 1.0
            col[k, 6 + i, 28] = 1.0
            row[k, 6 + i, 16 + 4 * i + k] = 1.0
    return np.concatenate([col.reshape(64, 32), row.reshape(64, 32)], axis=0)


def upward_packet(probes_t, basis_t, moves_t):
    leaves = [
        dot_t(probes_t[:, k * LEAF : (k + 1) * LEAF], basis_t[:, k * LEAF : (k + 1) * LEAF])
        for k in range(4)
    ]
    leaf = jnp.concatenate(leaves, axis=1).astype(BF16)
    mids = [
        dot_t(leaf[:, j * 128 : (j + 1) * 128], moves_t[:, j * 128 : (j + 1) * 128])
        for j in range(2)
    ]
    mid = jnp.concatenate(mids, axis=1).astype(BF16)
    top = dot_t(mid, moves_t[:, 256:384]).astype(BF16)
    halves = jnp.concatenate([top[:32], top[32:]], axis=1)
    halves = jnp.concatenate([halves, halves], axis=0)
    return jnp.concatenate([leaf, mid, halves], axis=1)


def matern(square):
    square = jnp.maximum(square, 1e-30)
    dist = square * lax.rsqrt(square)
    return (1.0 + RATE * dist) * jnp.exp2(dist * (-RATE2))


def split_dot(a, b):
    high = a.astype(BF16)
    low = (a - high.astype(F32)).astype(BF16)
    both = dot_n(jnp.concatenate([high, low], axis=0), b)
    return both[: a.shape[0]] + both[a.shape[0] :]


def features(sel, geo):
    flat = geo.astype(F32)
    squares = flat * flat
    norm = squares[0:4] + squares[4:8] + squares[8:12]
    high = norm.astype(BF16).astype(F32)
    rest = norm - high
    middle = rest.astype(BF16).astype(F32)
    low = rest - middle
    stack = jnp.concatenate([flat, high, middle, low, jnp.ones_like(norm)], axis=0)
    return dot_n(sel, stack.astype(BF16)).astype(BF16)


def packed(points, skeleton):
    pts = points.astype(F32)
    skel = skeleton.astype(F32)
    rows = []
    for i in range(3):
        for k in range(4):
            tail = skel[i : i + 1, k * 128 : min(k * 128 + 128, 448)]
            if k == 3:
                tail = jnp.concatenate([tail, jnp.zeros((1, 64), F32)], axis=1)
            rows.append(jnp.concatenate([pts[i : i + 1, k * LEAF : (k + 1) * LEAF], tail], axis=1))
    rows.append(jnp.zeros((4, GEO), F32))
    return jnp.concatenate(rows, axis=0).astype(BF16)


def chain(targets, live):
    across = jnp.broadcast_to(targets, (128, 128))
    down = across.T
    row = lax.broadcasted_iota(jnp.int32, (128, 128), 0)
    lane = lax.broadcasted_iota(jnp.int32, (128, 128), 1)
    prev = jnp.where((across == down) & (row < lane), row + 1, 0)
    last = jnp.where((down == lane) & (row < live), row + 1, 0)
    return jnp.max(prev, axis=0, keepdims=True), jnp.max(last, axis=0, keepdims=True)


def slot_tables(near_list, near_live, far_list, far_live):
    near = jnp.concatenate([near_list, jnp.zeros((2, 64), jnp.int32)], axis=1)
    target = jnp.clip(near[0:1], 0, 4 * N_COL - 1)
    source = jnp.clip(near[1:2], 0, 4 * N_ROW - 1)
    far_target = jnp.clip(far_list[0:1], 0, 7 * N_COL - 1)
    far_source = jnp.clip(far_list[1:2], 0, 7 * N_ROW - 1)
    far = jnp.concatenate([far_target, far_source], axis=0)
    device = (far * 9363) >> 16
    local = far - device * 7
    half = local >> 1
    odd = (local - half * 2).astype(F32)
    place = device * 4 + half
    index = jnp.concatenate(
        [target, source, *chain(target, near_live), place, *chain(far_target, far_live)], axis=0
    )
    weights = jnp.concatenate([1.0 - odd[0:1], odd[0:1], 1.0 - odd[1:2], odd[1:2]], axis=0)
    return index, jnp.concatenate([weights, jnp.zeros((4, 128), F32)], axis=0)


ORDER = (
    "a0", "pk", "g0", "b0", "a10", "up", "q0", "gz", "by1", "az1", "gy1", "qz1", "T", "by2", "gy2", "W", "q13",
    "q10", "qz2", "by3", "gy3", "bz0", "q11", "az2", "bz1", "gr", "q12", "q20", "q23", "bz2", "gy4", "F0", "F1",
    "q21", "K0", "K2", "q22", "K3", "a13", "N4", "a11", "N0", "q33", "q30", "q31", "N7", "N2", "q32", "by4",
    "a12", "N6", "a20", "bz3", "a23", "K1", "a21", "q40", "q43", "q42", "q41", "U", "M0", "a22", "M1", "M2",
    "a30", "M3", "fs", "a33", "a31", "N1", "a32", "bz4", "xf", "a40", "N5", "N3", "a43", "a42", "a41", "na", "sa",
    "be", "nb", "sb", "xa", "cf", "xb", "sw", "ef", "ca", "ea", "eb",
)


def main_kernel(
    order,
    near_count, far_count, near_any, far_any, sel_any, points_any, skeleton_any, probes_any, basis_any,
    moves_any,
    out_any,
    near_list, far_list, sel, points, skeleton, basis_t, moves_t, out, in_sems, out_sems,
    geo, index_v, index, weight_v, weight, table_sems,
    all_a, all_b, all_q, col_geo, row_geo, col_leaf, row_leaf, col_skel, row_skel,
    near_k, far_k, near_ca, near_cb, far_c, near_out, far_out,
    near_sib, far_sib, near_sum, far_sum, near_in, far_in, far_part,
    send, recv_a, recv_b, recv_q, geo_send, geo_recv, row_sems, ring_send, ring_recv, sems, sib_sems,
):
    r = lax.axis_index("row")
    c = lax.axis_index("col")
    zh = lax.div(r, N_Y)
    y = lax.rem(r, N_Y)
    core = lax.rem(c, 2)
    chip = lax.div(c, 2)
    sibling = chip * 2 + 1 - core
    z_lo = lax.div(chip, 4)
    x = lax.rem(chip, 4)

    def slot(dz, dy):
        return lax.rem(zh + dz, N_ZH) * N_Y + lax.rem(y + dy % N_Y, N_Y)

    up, down, across = slot(1, 0), slot(3, 0), slot(2, 0)
    right, left = slot(0, 1), slot(0, -1)
    me = slot(0, 0)

    barrier = pltpu.get_barrier_semaphore()
    for row in (up, down, across, right, left):
        pl.semaphore_signal(barrier, inc=1, device_id=(row, c), device_id_type=MESH)

    @pl.loop(1, N_COL)
    def _(d):
        pl.semaphore_signal(
            barrier, inc=1, device_id=(r, (c + d) % N_COL), device_id_type=MESH
        )

    loads = {
        name: pltpu.make_async_copy(src, dst, in_sems.at[i])
        for i, (name, src, dst) in enumerate(
            (
                ("points", points_any, points),
                ("skeleton", skeleton_any, skeleton),
                ("basis", basis_any, basis_t),
                ("moves", moves_any, moves_t),
                ("near", near_any, near_list),
                ("far", far_any, far_list),
                ("sel", sel_any, sel),
            )
        )
    }
    own = []
    for h, buf in enumerate((all_a, all_b)):
        for k in range(4):
            piece = probes_any.at[pl.ds(32 * h, 32), pl.ds(k * LEAF, LEAF)]
            own.append(pltpu.make_async_copy(piece, buf.at[me * 4 + k], in_sems.at[7 + 4 * h + k]))
    for one in own:
        one.start()
    for one in loads.values():
        one.start()
    for one in own:
        one.wait()
    pl.semaphore_wait(barrier, 5 + N_COL - 1)

    sends = []
    started = []
    unsent = []

    def send_later(first, last, copy_of):
        def waits():
            @pl.loop(first, last)
            def _(d):
                copy_of(d).wait_send()

        unsent.append(waits)

    def copy(src, dst, sem, row):
        one = pltpu.make_async_remote_copy(
            src_ref=src, dst_ref=dst, send_sem=send.at[len(started)], recv_sem=sem,
            device_id=(row, c), device_id_type=MESH,
        )
        one.start()
        sends.append(one)
        started.append(one)

    def arrived(dst, sem):
        pltpu.make_async_remote_copy(
            src_ref=dst, dst_ref=dst, send_sem=send.at[0], recv_sem=sem,
            device_id=(right, c), device_id_type=MESH,
        ).wait_recv()

    def mover(buf, sems, pitch, parts):
        def block(s, h=None):
            at = 0 if h != 1 else parts[0]
            return buf.at[pl.ds(s * pitch + at, sum(parts) if h is None else parts[h])]

        def push(s, row, h=None):
            copy(block(s, h), block(s, h), sems.at[s, h or 0], row)

        def wait(s, h=None):
            arrived(block(s, h), sems.at[s, h or 0])

        return push, wait

    movers = {
        "a": mover(all_a, recv_a, 4, (2, 2)),
        "b": mover(all_b, recv_b, 4, (2, 2)),
        "q": mover(all_q, recv_q, 8, (4, 3)),
    }

    def ring(name, dz, k):
        push, wait = movers[name]
        if k == 4:
            wait(slot(dz, 4), 0)
            wait(slot(dz, 4), 1)
            return
        wait(slot(dz, -k))
        push(slot(dz, -k), right, 0 if k == 3 else None)
        wait(slot(dz, k))
        push(slot(dz, k), left, 1 if k == 3 else None)

    def turn(name, dy):
        push, wait = movers[name]
        wait(slot(3, dy))
        push(slot(3, dy), up, 0)
        wait(slot(1, dy))
        push(slot(1, dy), down, 1)

    def geo_z(d):
        return pltpu.make_async_remote_copy(
            src_ref=geo, dst_ref=col_geo.at[y, zh],
            send_sem=geo_send.at[d], recv_sem=geo_recv.at[d],
            device_id=(slot(d, 0), c), device_id_type=MESH,
        )

    def geo_y(k, way):
        place = (y - k) % N_Y if way == 0 else (y + k) % N_Y
        return pltpu.make_async_remote_copy(
            src_ref=col_geo.at[place], dst_ref=col_geo.at[place],
            send_sem=ring_send.at[way, k], recv_sem=ring_recv.at[way, k],
            device_id=(right if way == 0 else left, c), device_id_type=MESH,
        )

    def geo_y_wait(k, way):
        place = (y - k - 1) % N_Y if way == 0 else (y + k + 1) % N_Y
        arrived(col_geo.at[place], ring_recv.at[way, k])

    def geo_row(d):
        return pltpu.make_async_remote_copy(
            src_ref=geo, dst_ref=row_geo.at[c],
            send_sem=row_sems.at[0, d], recv_sem=row_sems.at[1, d],
            device_id=(r, (c + d) % N_COL), device_id_type=MESH,
        )

    outs = (near_out.at[0], near_out.at[1], far_out)
    sibs = (near_sib.at[0], near_sib.at[1], far_sib)
    whole = (near_sum.at[0], near_sum.at[1], far_sum)
    comes = (near_in.at[0], near_in.at[1], far_in)

    def sib_copy(what, d):
        return pltpu.make_async_remote_copy(
            src_ref=outs[what].at[d], dst_ref=sibs[what].at[d],
            send_sem=sib_sems.at[2 * what, d], recv_sem=sib_sems.at[2 * what + 1, d],
            device_id=(r, sibling), device_id_type=MESH,
        )

    def chip_at(d):
        return lax.rem(z_lo + lax.div(d, 4), 2) * 4 + lax.rem(x + lax.rem(d, 4), 4)

    def chip_copy(what, d, by_x=False):
        to = chip_at(lax.rem(d, 4) if by_x else d)
        return pltpu.make_async_remote_copy(
            src_ref=whole[what].at[d], dst_ref=comes[what].at[d],
            send_sem=sems.at[2 * what, d], recv_sem=sems.at[2 * what + 1, d],
            device_id=(r, to * 2 + core), device_id_type=MESH,
        )

    def core_sum(what, d):
        sib_copy(what, d).wait_recv()
        owner = chip_at(d) * 2 + core
        if what == 2:
            far_sum[d] = (far_whole(owner) + far_sib[d].astype(F32)).astype(BF16)
            return
        for k in range(4):
            lanes = slice(k * LEAF, (k + 1) * LEAF)
            theirs = near_sib[what, d, :, lanes].astype(F32)
            near_sum[what, d, :, lanes] = (near_leaf(what, owner, k) + theirs).astype(BF16)

    def spread(what):
        @pl.loop(0, 7)
        def _(i):
            core_sum(what, 7 - i)
            chip_copy(what, 7 - i).start()

        send_later(1, 8, functools.partial(chip_copy, what))

    def spread_x(what):
        for first in (5, 1):

            @pl.loop(0, 3)
            def _(i):
                d = first + 2 - i
                core_sum(what, d)
                chip_copy(what, d, True).start()

            send_later(first, first + 3, functools.partial(chip_copy, what, by_x=True))

        core_sum(what, 4)

    def cross(what):
        total = whole[what][4].astype(F32)
        for d in (5, 6, 7):
            chip_copy(what, d, True).wait_recv()
            total = total + comes[what][d].astype(F32)
        whole[what][4] = total.astype(BF16)
        chip_copy(what, 4).start()
        send_later(4, 5, functools.partial(chip_copy, what))

    def near_leaf(h, owner, k):
        return (near_ca, near_cb)[h][index[3, owner * 4 + k]]

    def far_whole(owner):
        parts = [far_c[index[7, owner * 7 + j]] for j in range(7)] + [jnp.zeros((64, 64), F32)]
        return jnp.concatenate(parts, axis=1)

    stores = [
        pltpu.make_async_copy(
            out.at[pl.ds(32 * h, 32)], out_any.at[pl.ds(32 * h, 32)], out_sems.at[h]
        )
        for h in range(2)
    ]
    tables = (
        pltpu.make_async_copy(index_v, index, table_sems.at[0]),
        pltpu.make_async_copy(weight_v, weight, table_sems.at[1]),
    )

    def event(e):
        if e == "pk":
            loads["points"].wait()
            loads["skeleton"].wait()
            geo[...] = packed(points[...], skeleton[...])
            col_geo[y, zh] = geo[...]
            row_geo[c] = geo[...]
        elif e == "sw":
            while sends:
                sends.pop().wait_send()
            while unsent:
                unsent.pop()()
        elif e == "g0":
            for d in (1, 2, 3):
                geo_z(d).start()

            @pl.loop(1, N_COL)
            def _(d):
                geo_row(d).start()

            send_later(1, 4, geo_z)
            send_later(1, N_COL, geo_row)

        elif e == "up":
            loads["basis"].wait()
            loads["moves"].wait()
            probes_t = jnp.concatenate(
                [
                    jnp.concatenate([buf[me * 4 + k] for k in range(4)], axis=1)
                    for buf in (all_a, all_b)
                ],
                axis=0,
            )
            packet = upward_packet(probes_t, basis_t[...], moves_t[...])
            for j in range(7):
                rows = slice((j % 2) * 32, (j % 2) * 32 + 32)
                all_q[me * 8 + j] = packet[rows, (j // 2) * 128 : (j // 2) * 128 + 128]
        elif e in ("a0", "b0", "q0"):
            for row in (right, left, up, down) if e == "b0" else (up, down, right, left):
                movers[e[0]][0](me, row)
        elif e == "gz":
            for d in (1, 2, 3):
                arrived(col_geo.at[y, (zh - d) % N_ZH], geo_recv.at[d])
            geo_y(0, 0).start()
            geo_y(0, 1).start()
            send_later(0, 4, lambda k: geo_y(k, 0))
            send_later(0, 3, lambda k: geo_y(k, 1))
        elif e in ("gy1", "gy2", "gy3", "gy4"):
            k = int(e[2])
            geo_y_wait(k - 1, 0)
            if k < 4:
                geo_y(k, 0).start()
                geo_y_wait(k - 1, 1)
                if k < 3:
                    geo_y(k, 1).start()
        elif e in ("az1", "qz1"):
            turn(e[0], 0)
            for dz in (3, 1):
                movers[e[0]][0](slot(dz, 0), right)
                movers[e[0]][0](slot(dz, 0), left)
        elif e in ("az2", "qz2"):
            push, wait = movers[e[0]]
            wait(slot(2, 0), 0)
            wait(slot(2, 0), 1)
            push(slot(2, 0), right)
            push(slot(2, 0), left)
        elif e[0] in "aq":
            ring(e[0], int(e[2]), int(e[1]))
        elif e[:2] == "by":
            k = int(e[2])
            ring("b", 0, k)
            for dy in (-k, k) if k < 4 else (4,):
                movers["b"][0](slot(0, dy), up)
                movers["b"][0](slot(0, dy), down)
        elif e[:2] == "bz":
            k = int(e[2])
            for dy in (-k, k) if 0 < k < 4 else (k,):
                turn("b", dy)
        elif e == "be":
            for dy in (0, -1, 1, -2, 2, -3, 3, 4):
                movers["b"][1](slot(2, dy), 0)
                movers["b"][1](slot(2, dy), 1)
        elif e == "gr":

            @pl.loop(1, N_COL)
            def _(d):
                arrived(row_geo.at[(c + N_COL - d) % N_COL], row_sems.at[1, d])

        elif e[0] == "F":
            part = int(e[1])
            if part == 0:
                loads["sel"].wait()

            @pl.loop(part * 4, part * 4 + 4)
            def _(j):
                wide = jnp.concatenate([col_geo[j, k] for k in range(N_ZH)], axis=1)
                feat = features(sel[0:64], wide)
                for k in range(N_ZH):
                    store_features(col_leaf, col_skel, k * N_Y + j, feat[:, k * GEO : (k + 1) * GEO])

            @pl.loop(part * 2, part * 2 + 2)
            def _(j):
                wide = jnp.concatenate([row_geo[j * 4 + k] for k in range(4)], axis=1)
                feat = features(sel[64:128], wide)
                for k in range(4):
                    store_features(row_leaf, row_skel, j * 4 + k, feat[:, k * GEO : (k + 1) * GEO])

        elif e[0] == "N":
            for u in range(8):
                s = int(e[1]) * 8 + u
                square = dot_l(col_leaf[index[1, s]], row_leaf[index[0, s]])
                near_k[s] = matern(square).astype(BF16)
        elif e[0] == "K":

            @pl.loop(int(e[1]) * 2, int(e[1]) * 2 + 2)
            def _(g):
                for u in range(16):
                    s = g * 16 + u
                    ours = one_of(col_skel[index[5, s]], weight[2, s], weight[3, s])
                    theirs = one_of(row_skel[index[4, s]], weight[0, s], weight[1, s])
                    kern = matern(dot_l(ours, theirs))
                    far_k[s, 0:64] = (kern * weight[2, s]).astype(BF16)
                    far_k[s, 64:128] = (kern * weight[3, s]).astype(BF16)

        elif e == "U":
            far_c[0] = jnp.zeros((64, 64), F32)

            @pl.loop(0, N_ROW // 4)
            def _(g):
                for u in range(4):
                    d = g * 4 + u
                    top = all_q[d * 8 + 6]
                    all_q[d * 8 + 7] = jnp.concatenate([top[:, 64:], top[:, :64]], axis=1)

        elif e[0] == "M":

            @pl.loop(int(e[1]) * 2, int(e[1]) * 2 + 2)
            def _(g):
                for u in range(16):
                    s = g * 16 + u
                    at = index[5, s] * 2
                    pair = jnp.concatenate([all_q[at], all_q[at + 1]], axis=0)
                    far_c[s + 1] = far_c[index[6, s]] + dot_n(pair, far_k[s])

        elif e == "fs":

            @pl.loop(0, 8)
            def _(i):
                d = 7 - i
                far_out[d] = far_whole(chip_at(d) * 2 + 1 - core).astype(BF16)
                sib_copy(2, d).start()

            send_later(0, 8, functools.partial(sib_copy, 2))

        elif e in ("xa", "xf"):
            spread_x(0 if e == "xa" else 2)
        elif e in ("ca", "cf"):
            cross(0 if e == "ca" else 2)
        elif e == "xb":
            spread(1)
        elif e in ("na", "nb"):
            sums, samples = (near_ca, all_a) if e == "na" else (near_cb, all_b)
            sums[0] = jnp.zeros((32, LEAF), F32)

            @pl.loop(0, NEAR_MOST // 16)
            def _(g):
                for u in range(16):
                    s = g * 16 + u
                    sums[s + 1] = sums[index[2, s]] + dot_n(samples[index[1, s]], near_k[s])

        elif e in ("sa", "sb"):
            h = "ab".index(e[1])

            @pl.loop(0, 8)
            def _(i):
                d = 7 - i
                owner = chip_at(d) * 2 + 1 - core
                for k in range(4):
                    near_out[h, d, :, k * LEAF : (k + 1) * LEAF] = near_leaf(h, owner, k).astype(BF16)
                sib_copy(h, d).start()

            send_later(0, 8, functools.partial(sib_copy, h))
        elif e == "ef":
            sib_copy(2, 0).wait_recv()
            total = far_whole(c) + far_sib[0].astype(F32)
            for d in range(1, 5):
                chip_copy(2, d).wait_recv()
                total = total + far_in[d].astype(F32)
            middle = total[:, 256:384] + split_dot(total[:, 384:448], moves_t[:, 256:384])
            for k in range(4):
                leaf = total[:, k * 64 : (k + 1) * 64] + split_dot(
                    middle[:, (k // 2) * 64 : (k // 2) * 64 + 64], moves_t[:, k * 64 : (k + 1) * 64]
                )
                lanes = slice(k * LEAF, (k + 1) * LEAF)
                far_part[:, lanes] = split_dot(leaf, basis_t[:, lanes])
        elif e in ("ea", "eb"):
            h = "ab".index(e[1])
            rows = slice(32 * h, 32 * h + 32)
            sib_copy(h, 0).wait_recv()
            others = range(1, 5) if h == 0 else range(1, 8)
            for d in others:
                chip_copy(h, d).wait_recv()
            for k in range(4):
                lanes = slice(k * LEAF, (k + 1) * LEAF)
                total = near_leaf(h, c, k) + near_sib[h, 0, :, lanes].astype(F32) + far_part[rows, lanes]
                for d in others:
                    total = total + near_in[h, d, :, lanes].astype(F32)
                out[rows, lanes] = total.astype(BF16)
            stores[h].start()
        elif e == "T":
            loads["near"].wait()
            loads["far"].wait()
            index_v[...], weight_v[...] = slot_tables(
                near_list[...], near_count[0, 0], far_list[...], far_count[0, 0]
            )
            for one in tables:
                one.start()
        elif e == "W":
            for one in tables:
                one.wait()
        else:
            raise ValueError(e)

    def store_features(leaf, skel, d, feat):
        leaf[pl.ds(d * 4, 4)] = feat[:, 0:256].reshape(4, 16, 256)
        skel[pl.ds(d * 4, 4)] = feat[:, 256:384].reshape(4, 16, 128)

    def one_of(pair, first, second):
        pair = pair.astype(F32)
        return (pair[:, :64] * first + pair[:, 64:] * second).astype(BF16)

    for e in order:
        event(e)

    event("sw")
    for one in stores:
        one.wait()


def run(near_count, far_count, near_list, far_list, sel, points, skeleton, probes_t, basis_t, moves_t):
    smem = pl.BlockSpec(memory_space=pltpu.SMEM)
    dma = pltpu.SemaphoreType.DMA
    return pl.pallas_call(
        functools.partial(main_kernel, ORDER),
        out_shape=jax.ShapeDtypeStruct((64, 1024), BF16),
        in_specs=[smem] * 2 + [pl.BlockSpec(memory_space=pl.ANY)] * 8,
        out_specs=pl.BlockSpec(memory_space=pl.ANY),
        scratch_shapes=[
            pltpu.VMEM((2, NEAR_MOST), jnp.int32),
            pltpu.VMEM((2, FAR_MOST), jnp.int32),
            pltpu.VMEM((128, 32), BF16),
            pltpu.VMEM((3, 4 * LEAF), BF16),
            pltpu.VMEM((3, 7 * RANK), BF16),
            pltpu.VMEM((64, 4 * LEAF), BF16),
            pltpu.VMEM((64, 6 * RANK), BF16),
            pltpu.VMEM((64, 4 * LEAF), BF16),
            dma((15,)),
            dma((2,)),
            pltpu.VMEM((16, GEO), BF16),
            pltpu.VMEM((8, 128), jnp.int32),
            pltpu.SMEM((8, 128), jnp.int32),
            pltpu.VMEM((8, 128), F32),
            pltpu.SMEM((8, 128), F32),
            dma((2,)),
            pltpu.VMEM((4 * N_ROW, 32, LEAF), BF16),
            pltpu.VMEM((4 * N_ROW, 32, LEAF), BF16),
            pltpu.VMEM((8 * N_ROW, 32, 128), BF16),
            pltpu.VMEM((N_Y, N_ZH, 16, GEO), BF16),
            pltpu.VMEM((N_COL, 16, GEO), BF16),
            pltpu.VMEM((4 * N_ROW, 16, LEAF), BF16),
            pltpu.VMEM((4 * N_COL, 16, LEAF), BF16),
            pltpu.VMEM((4 * N_ROW, 16, 128), BF16),
            pltpu.VMEM((4 * N_COL, 16, 128), BF16),
            pltpu.VMEM((NEAR_MOST, LEAF, LEAF), BF16),
            pltpu.VMEM((FAR_MOST, 2 * RANK, RANK), BF16),
            pltpu.VMEM((NEAR_MOST + 1, 32, LEAF), F32),
            pltpu.VMEM((NEAR_MOST + 1, 32, LEAF), F32),
            pltpu.VMEM((FAR_MOST + 1, SAMPLES, RANK), F32),
            pltpu.VMEM((2, 8, 32, 1024), BF16),
            pltpu.VMEM((8, 64, 512), BF16),
            pltpu.VMEM((2, 8, 32, 1024), BF16),
            pltpu.VMEM((8, 64, 512), BF16),
            pltpu.VMEM((2, 8, 32, 1024), BF16),
            pltpu.VMEM((8, 64, 512), BF16),
            pltpu.VMEM((2, 8, 32, 1024), BF16),
            pltpu.VMEM((8, 64, 512), BF16),
            pltpu.VMEM((64, 1024), F32),
            dma((120,)),
            dma((N_ROW, 2)),
            dma((N_ROW, 2)),
            dma((N_ROW, 2)),
            dma((4,)),
            dma((4,)),
            dma((2, N_COL)),
            dma((2, 4)),
            dma((2, 4)),
            dma((6, 8)),
            dma((6, 8)),
        ],
        compiler_params=pltpu.CompilerParams(
            collective_id=0, has_side_effects=True, vmem_limit_bytes=56 << 20
        ),
        name="sample",
    )(near_count, far_count, near_list, far_list, sel, points, skeleton, probes_t, basis_t, moves_t)


def local(
    probes, points, skeleton, leaf_basis, transfer, near_list, near_count, far_list, far_count
):
    sel = jnp.asarray(selections(), BF16)
    return run(
        near_count, far_count, near_list[0, 0], far_list[0, 0],
        sel, points, skeleton, probes.T, leaf_basis.T, transfer.T,
    ).T


def solution(mesh):
    placed = (
        P(("row", "col"), None),
        P(None, ("row", "col")),
        P(None, ("row", "col")),
        P(("row", "col"), None),
        P(("row", "col"), None),
        P("row", "col", None, None),
        P("row", "col"),
        P("row", "col", None, None),
        P("row", "col"),
    )
    return jax.shard_map(
        local, mesh=mesh, in_specs=placed, out_specs=P(("row", "col"), None), check_vma=False
    )
```

```python
import functools
import math

import jax
import jax.numpy as jnp
import numpy as np
from jax import lax
from jax.experimental import pallas as pl
from jax.experimental.pallas import tpu as pltpu
from jax.sharding import PartitionSpec as P

LEAF = 256
RANK = 64
SAMPLES = 64
N_ROW = 32
N_COL = 16
N_Y = 8
N_ZH = 4
NEAR_MOST = 64
FAR_MOST = 128
GEO = 384
MESH = pl.DeviceIdType.MESH
F32 = jnp.float32
BF16 = jnp.bfloat16
RATE = math.sqrt(3.0) / 0.15
RATE2 = RATE * math.log2(math.e)


def dot_t(a, b):
    return lax.dot_general(a, b, (((1,), (1,)), ((), ())), preferred_element_type=F32)


def dot_l(a, b):
    return lax.dot_general(a, b, (((0,), (0,)), ((), ())), preferred_element_type=F32)


def dot_n(a, b):
    return jnp.dot(a, b, preferred_element_type=F32)


def selections():
    col = np.zeros((4, 16, 32), np.float32)
    row = np.zeros((4, 16, 32), np.float32)
    for k in range(4):
        for i in range(3):
            col[k, i, i * 4 + k] = -2.0
            row[k, i, i * 4 + k] = 1.0
            col[k, 3 + i, 16 + 4 * i + k] = 1.0
            row[k, 3 + i, 28] = 1.0
            col[k, 6 + i, 28] = 1.0
            row[k, 6 + i, 16 + 4 * i + k] = 1.0
    return np.concatenate([col.reshape(64, 32), row.reshape(64, 32)], axis=0)


def upward_packet(probes_t, basis_t, moves_t):
    leaves = [
        dot_t(probes_t[:, k * LEAF : (k + 1) * LEAF], basis_t[:, k * LEAF : (k + 1) * LEAF])
        for k in range(4)
    ]
    leaf = jnp.concatenate(leaves, axis=1).astype(BF16)
    mids = [
        dot_t(leaf[:, j * 128 : (j + 1) * 128], moves_t[:, j * 128 : (j + 1) * 128])
        for j in range(2)
    ]
    mid = jnp.concatenate(mids, axis=1).astype(BF16)
    top = dot_t(mid, moves_t[:, 256:384]).astype(BF16)
    halves = jnp.concatenate([top[:32], top[32:]], axis=1)
    halves = jnp.concatenate([halves, halves], axis=0)
    return jnp.concatenate([leaf, mid, halves], axis=1)


def matern(square):
    square = jnp.maximum(square, 1e-30)
    dist = square * lax.rsqrt(square)
    return (1.0 + RATE * dist) * jnp.exp2(dist * (-RATE2))


def split_dot(a, b):
    high = a.astype(BF16)
    low = (a - high.astype(F32)).astype(BF16)
    both = dot_n(jnp.concatenate([high, low], axis=0), b)
    return both[: a.shape[0]] + both[a.shape[0] :]


def features(sel, geo):
    flat = geo.astype(F32)
    squares = flat * flat
    norm = squares[0:4] + squares[4:8] + squares[8:12]
    high = norm.astype(BF16).astype(F32)
    rest = norm - high
    middle = rest.astype(BF16).astype(F32)
    low = rest - middle
    stack = jnp.concatenate([flat, high, middle, low, jnp.ones_like(norm)], axis=0)
    return dot_n(sel, stack.astype(BF16)).astype(BF16)


def packed(points, skeleton):
    pts = points.astype(F32)
    skel = skeleton.astype(F32)
    rows = []
    for i in range(3):
        for k in range(4):
            tail = skel[i : i + 1, k * 128 : min(k * 128 + 128, 448)]
            if k == 3:
                tail = jnp.concatenate([tail, jnp.zeros((1, 64), F32)], axis=1)
            rows.append(jnp.concatenate([pts[i : i + 1, k * LEAF : (k + 1) * LEAF], tail], axis=1))
    rows.append(jnp.zeros((4, GEO), F32))
    return jnp.concatenate(rows, axis=0).astype(BF16)


def chain(targets, live):
    across = jnp.broadcast_to(targets, (128, 128))
    down = across.T
    row = lax.broadcasted_iota(jnp.int32, (128, 128), 0)
    lane = lax.broadcasted_iota(jnp.int32, (128, 128), 1)
    prev = jnp.where((across == down) & (row < lane), row + 1, 0)
    last = jnp.where((down == lane) & (row < live), row + 1, 0)
    return jnp.max(prev, axis=0, keepdims=True), jnp.max(last, axis=0, keepdims=True)


def slot_tables(near_list, near_live, far_list, far_live):
    near = jnp.concatenate([near_list, jnp.zeros((2, 64), jnp.int32)], axis=1)
    target = jnp.clip(near[0:1], 0, 4 * N_COL - 1)
    source = jnp.clip(near[1:2], 0, 4 * N_ROW - 1)
    far_target = jnp.clip(far_list[0:1], 0, 7 * N_COL - 1)
    far_source = jnp.clip(far_list[1:2], 0, 7 * N_ROW - 1)
    far = jnp.concatenate([far_target, far_source], axis=0)
    device = (far * 9363) >> 16
    local = far - device * 7
    half = local >> 1
    odd = (local - half * 2).astype(F32)
    place = device * 4 + half
    index = jnp.concatenate(
        [target, source, *chain(target, near_live), place, *chain(far_target, far_live)], axis=0
    )
    weights = jnp.concatenate([1.0 - odd[0:1], odd[0:1], 1.0 - odd[1:2], odd[1:2]], axis=0)
    return index, jnp.concatenate([weights, jnp.zeros((4, 128), F32)], axis=0)


ORDER = (
    "pk", "g0", "a0", "b0", "up", "q0", "gz", "a10", "q10", "gy1", "qz1", "by1", "gy2", "q13", "gr", "qz2", "bz0",
    "T", "by2", "gy3", "q11", "q20", "q12", "az1", "gy4", "W", "F0", "by3", "F1", "q23", "q21", "K1", "q22", "N0",
    "K0", "az2", "N4", "q30", "N5", "a11", "bz1", "N1", "q33", "q31", "bz2", "q32", "bz3", "a12", "a13", "by4",
    "K3", "K2", "a20", "a21", "q43", "N6", "q42", "q40", "q41", "U", "M0", "a22", "M1", "a23", "M2", "M3", "a30",
    "fs", "a31", "a32", "N3", "a33", "bz4", "xf", "N7", "N2", "a41", "a40", "a43", "a42", "na", "sa", "be", "nb",
    "xa", "sb", "cf", "xb", "ca", "sw", "ef", "ea", "eb",
)


def main_kernel(
    order,
    near_count, far_count, near_any, far_any, sel_any, points_any, skeleton_any, probes_any, basis_any,
    moves_any,
    out_any,
    near_list, far_list, sel, points, skeleton, basis_t, moves_t, out, in_sems, out_sems,
    geo, index_v, index, weight_v, weight, table_sems,
    all_a, all_b, all_q, col_geo, row_geo, col_leaf, row_leaf, col_skel, row_skel,
    near_k, far_k, near_ca, near_cb, far_c, near_out, far_out,
    near_sib, far_sib, near_sum, far_sum, near_in, far_in, far_part,
    send, recv_a, recv_b, recv_q, geo_send, geo_recv, row_sems, ring_send, ring_recv, sems, sib_sems,
):
    r = lax.axis_index("row")
    c = lax.axis_index("col")
    zh = lax.div(r, N_Y)
    y = lax.rem(r, N_Y)
    core = lax.rem(c, 2)
    chip = lax.div(c, 2)
    sibling = chip * 2 + 1 - core
    z_lo = lax.div(chip, 4)
    x = lax.rem(chip, 4)

    def slot(dz, dy):
        return lax.rem(zh + dz, N_ZH) * N_Y + lax.rem(y + dy % N_Y, N_Y)

    up, down, across = slot(1, 0), slot(3, 0), slot(2, 0)
    right, left = slot(0, 1), slot(0, -1)
    me = slot(0, 0)

    barrier = pltpu.get_barrier_semaphore()
    for row in (up, down, across, right, left):
        pl.semaphore_signal(barrier, inc=1, device_id=(row, c), device_id_type=MESH)

    @pl.loop(1, N_COL)
    def _(d):
        pl.semaphore_signal(
            barrier, inc=1, device_id=(r, (c + d) % N_COL), device_id_type=MESH
        )

    loads = {
        name: pltpu.make_async_copy(src, dst, in_sems.at[i])
        for i, (name, src, dst) in enumerate(
            (
                ("points", points_any, points),
                ("skeleton", skeleton_any, skeleton),
                ("basis", basis_any, basis_t),
                ("moves", moves_any, moves_t),
                ("near", near_any, near_list),
                ("far", far_any, far_list),
                ("sel", sel_any, sel),
            )
        )
    }
    own = []
    for h, buf in enumerate((all_a, all_b)):
        for k in range(4):
            piece = probes_any.at[pl.ds(32 * h, 32), pl.ds(k * LEAF, LEAF)]
            own.append(pltpu.make_async_copy(piece, buf.at[me * 4 + k], in_sems.at[7 + 4 * h + k]))
    for one in own:
        one.start()
    for one in loads.values():
        one.start()
    for one in own:
        one.wait()
    pl.semaphore_wait(barrier, 5 + N_COL - 1)

    sends = []
    started = []
    unsent = []
    gathered = []

    def send_later(first, last, copy_of, held=unsent):
        def waits():
            @pl.loop(first, last)
            def _(d):
                copy_of(d).wait_send()

        held.append(waits)

    def copy(src, dst, sem, row):
        one = pltpu.make_async_remote_copy(
            src_ref=src, dst_ref=dst, send_sem=send.at[len(started)], recv_sem=sem,
            device_id=(row, c), device_id_type=MESH,
        )
        one.start()
        sends.append(one)
        started.append(one)

    def arrived(dst, sem):
        pltpu.make_async_remote_copy(
            src_ref=dst, dst_ref=dst, send_sem=send.at[0], recv_sem=sem,
            device_id=(right, c), device_id_type=MESH,
        ).wait_recv()

    def mover(buf, sems, pitch, parts):
        def block(s, h=None):
            at = 0 if h != 1 else parts[0]
            return buf.at[pl.ds(s * pitch + at, sum(parts) if h is None else parts[h])]

        def push(s, row, h=None):
            copy(block(s, h), block(s, h), sems.at[s, h or 0], row)

        def wait(s, h=None):
            arrived(block(s, h), sems.at[s, h or 0])

        return push, wait

    movers = {
        "a": mover(all_a, recv_a, 4, (2, 2)),
        "b": mover(all_b, recv_b, 4, (2, 2)),
        "q": mover(all_q, recv_q, 8, (4, 3)),
    }

    def ring(name, dz, k):
        push, wait = movers[name]
        if k == 4:
            wait(slot(dz, 4), 0)
            wait(slot(dz, 4), 1)
            return
        wait(slot(dz, -k))
        push(slot(dz, -k), right, 0 if k == 3 else None)
        wait(slot(dz, k))
        push(slot(dz, k), left, 1 if k == 3 else None)

    def turn(name, dy):
        push, wait = movers[name]
        wait(slot(3, dy))
        push(slot(3, dy), up, 0)
        wait(slot(1, dy))
        push(slot(1, dy), down, 1)

    def geo_z(d):
        return pltpu.make_async_remote_copy(
            src_ref=geo, dst_ref=col_geo.at[y, zh],
            send_sem=geo_send.at[d], recv_sem=geo_recv.at[d],
            device_id=(slot(d, 0), c), device_id_type=MESH,
        )

    def geo_y(k, way):
        place = (y - k) % N_Y if way == 0 else (y + k) % N_Y
        return pltpu.make_async_remote_copy(
            src_ref=col_geo.at[place], dst_ref=col_geo.at[place],
            send_sem=ring_send.at[way, k], recv_sem=ring_recv.at[way, k],
            device_id=(right if way == 0 else left, c), device_id_type=MESH,
        )

    def geo_y_wait(k, way):
        place = (y - k - 1) % N_Y if way == 0 else (y + k + 1) % N_Y
        arrived(col_geo.at[place], ring_recv.at[way, k])

    def geo_row(d):
        return pltpu.make_async_remote_copy(
            src_ref=geo, dst_ref=row_geo.at[c],
            send_sem=row_sems.at[0, d], recv_sem=row_sems.at[1, d],
            device_id=(r, (c + d) % N_COL), device_id_type=MESH,
        )

    outs = (near_out.at[0], near_out.at[1], far_out)
    sibs = (near_sib.at[0], near_sib.at[1], far_sib)
    whole = (near_sum.at[0], near_sum.at[1], far_sum)
    comes = (near_in.at[0], near_in.at[1], far_in)

    def sib_copy(what, d):
        return pltpu.make_async_remote_copy(
            src_ref=outs[what].at[d], dst_ref=sibs[what].at[d],
            send_sem=sib_sems.at[2 * what, d], recv_sem=sib_sems.at[2 * what + 1, d],
            device_id=(r, sibling), device_id_type=MESH,
        )

    def chip_at(d):
        return lax.rem(z_lo + lax.div(d, 4), 2) * 4 + lax.rem(x + lax.rem(d, 4), 4)

    def chip_copy(what, d, by_x=False):
        to = chip_at(lax.rem(d, 4) if by_x else d)
        return pltpu.make_async_remote_copy(
            src_ref=whole[what].at[d], dst_ref=comes[what].at[d],
            send_sem=sems.at[2 * what, d], recv_sem=sems.at[2 * what + 1, d],
            device_id=(r, to * 2 + core), device_id_type=MESH,
        )

    def core_sum(what, d):
        sib_copy(what, d).wait_recv()
        owner = chip_at(d) * 2 + core
        if what == 2:
            far_sum[d] = (far_whole(owner) + far_sib[d].astype(F32)).astype(BF16)
            return
        for k in range(4):
            lanes = slice(k * LEAF, (k + 1) * LEAF)
            theirs = near_sib[what, d, :, lanes].astype(F32)
            near_sum[what, d, :, lanes] = (near_leaf(what, owner, k) + theirs).astype(BF16)

    def spread(what):
        @pl.loop(0, 7)
        def _(i):
            core_sum(what, 7 - i)
            chip_copy(what, 7 - i).start()

        send_later(1, 8, functools.partial(chip_copy, what))

    def spread_x(what):
        for first in (5, 1):

            @pl.loop(0, 3)
            def _(i):
                d = first + 2 - i
                core_sum(what, d)
                chip_copy(what, d, True).start()

            send_later(first, first + 3, functools.partial(chip_copy, what, by_x=True))

        core_sum(what, 4)

    def cross(what):
        total = whole[what][4].astype(F32)
        for d in (5, 6, 7):
            chip_copy(what, d, True).wait_recv()
            total = total + comes[what][d].astype(F32)
        whole[what][4] = total.astype(BF16)
        chip_copy(what, 4).start()
        send_later(4, 5, functools.partial(chip_copy, what))

    def near_leaf(h, owner, k):
        return (near_ca, near_cb)[h][index[3, owner * 4 + k]]

    def far_whole(owner):
        parts = [far_c[index[7, owner * 7 + j]] for j in range(7)] + [jnp.zeros((64, 64), F32)]
        return jnp.concatenate(parts, axis=1)

    stores = [
        pltpu.make_async_copy(
            out.at[pl.ds(32 * h, 32)], out_any.at[pl.ds(32 * h, 32)], out_sems.at[h]
        )
        for h in range(2)
    ]
    tables = (
        pltpu.make_async_copy(index_v, index, table_sems.at[0]),
        pltpu.make_async_copy(weight_v, weight, table_sems.at[1]),
    )

    def event(e):
        if e == "pk":
            loads["points"].wait()
            loads["skeleton"].wait()
            geo[...] = packed(points[...], skeleton[...])
            col_geo[y, zh] = geo[...]
            row_geo[c] = geo[...]
        elif e == "sw":
            while sends:
                sends.pop().wait_send()
            while gathered:
                gathered.pop()()
        elif e == "g0":
            for d in (1, 2, 3):
                geo_z(d).start()

            @pl.loop(1, N_COL)
            def _(d):
                geo_row(d).start()

            send_later(1, 4, geo_z, gathered)
            send_later(1, N_COL, geo_row, gathered)

        elif e == "up":
            loads["basis"].wait()
            loads["moves"].wait()
            probes_t = jnp.concatenate(
                [
                    jnp.concatenate([buf[me * 4 + k] for k in range(4)], axis=1)
                    for buf in (all_a, all_b)
                ],
                axis=0,
            )
            packet = upward_packet(probes_t, basis_t[...], moves_t[...])
            for j in range(7):
                rows = slice((j % 2) * 32, (j % 2) * 32 + 32)
                all_q[me * 8 + j] = packet[rows, (j // 2) * 128 : (j // 2) * 128 + 128]
        elif e in ("a0", "b0", "q0"):
            for row in (right, left, up, down) if e == "b0" else (up, down, right, left):
                movers[e[0]][0](me, row)
        elif e == "gz":
            for d in (1, 2, 3):
                arrived(col_geo.at[y, (zh - d) % N_ZH], geo_recv.at[d])
            geo_y(0, 0).start()
            geo_y(0, 1).start()
            send_later(0, 4, lambda k: geo_y(k, 0), gathered)
            send_later(0, 3, lambda k: geo_y(k, 1), gathered)
        elif e in ("gy1", "gy2", "gy3", "gy4"):
            k = int(e[2])
            geo_y_wait(k - 1, 0)
            if k < 4:
                geo_y(k, 0).start()
                geo_y_wait(k - 1, 1)
                if k < 3:
                    geo_y(k, 1).start()
        elif e in ("az1", "qz1"):
            turn(e[0], 0)
            for dz in (3, 1):
                movers[e[0]][0](slot(dz, 0), right)
                movers[e[0]][0](slot(dz, 0), left)
        elif e in ("az2", "qz2"):
            push, wait = movers[e[0]]
            wait(slot(2, 0), 0)
            wait(slot(2, 0), 1)
            push(slot(2, 0), right)
            push(slot(2, 0), left)
        elif e[0] in "aq":
            ring(e[0], int(e[2]), int(e[1]))
        elif e[:2] == "by":
            k = int(e[2])
            ring("b", 0, k)
            for dy in (-k, k) if k < 4 else (4,):
                movers["b"][0](slot(0, dy), up)
                movers["b"][0](slot(0, dy), down)
        elif e[:2] == "bz":
            k = int(e[2])
            for dy in (-k, k) if 0 < k < 4 else (k,):
                turn("b", dy)
        elif e == "be":
            for dy in (0, -1, 1, -2, 2, -3, 3, 4):
                movers["b"][1](slot(2, dy), 0)
                movers["b"][1](slot(2, dy), 1)
        elif e == "gr":

            @pl.loop(1, N_COL)
            def _(d):
                arrived(row_geo.at[(c + N_COL - d) % N_COL], row_sems.at[1, d])

        elif e[0] == "F":
            part = int(e[1])
            if part == 0:
                loads["sel"].wait()

            @pl.loop(part * 4, part * 4 + 4)
            def _(j):
                wide = jnp.concatenate([col_geo[j, k] for k in range(N_ZH)], axis=1)
                feat = features(sel[0:64], wide)
                for k in range(N_ZH):
                    store_features(col_leaf, col_skel, k * N_Y + j, feat[:, k * GEO : (k + 1) * GEO])

            @pl.loop(part * 2, part * 2 + 2)
            def _(j):
                wide = jnp.concatenate([row_geo[j * 4 + k] for k in range(4)], axis=1)
                feat = features(sel[64:128], wide)
                for k in range(4):
                    store_features(row_leaf, row_skel, j * 4 + k, feat[:, k * GEO : (k + 1) * GEO])

        elif e[0] == "N":
            for u in range(8):
                s = int(e[1]) * 8 + u
                square = dot_l(col_leaf[index[1, s]], row_leaf[index[0, s]])
                near_k[s] = matern(square).astype(BF16)
        elif e[0] == "K":

            @pl.loop(int(e[1]) * 2, int(e[1]) * 2 + 2)
            def _(g):
                for u in range(16):
                    s = g * 16 + u
                    ours = one_of(col_skel[index[5, s]], weight[2, s], weight[3, s])
                    theirs = one_of(row_skel[index[4, s]], weight[0, s], weight[1, s])
                    kern = matern(dot_l(ours, theirs))
                    far_k[s, 0:64] = (kern * weight[2, s]).astype(BF16)
                    far_k[s, 64:128] = (kern * weight[3, s]).astype(BF16)

        elif e == "U":
            far_c[0] = jnp.zeros((64, 64), F32)

            @pl.loop(0, N_ROW // 4)
            def _(g):
                for u in range(4):
                    d = g * 4 + u
                    top = all_q[d * 8 + 6]
                    all_q[d * 8 + 7] = jnp.concatenate([top[:, 64:], top[:, :64]], axis=1)

        elif e[0] == "M":

            @pl.loop(int(e[1]) * 2, int(e[1]) * 2 + 2)
            def _(g):
                for u in range(16):
                    s = g * 16 + u
                    at = index[5, s] * 2
                    pair = jnp.concatenate([all_q[at], all_q[at + 1]], axis=0)
                    far_c[s + 1] = far_c[index[6, s]] + dot_n(pair, far_k[s])

        elif e == "fs":

            @pl.loop(0, 8)
            def _(i):
                d = 7 - i
                far_out[d] = far_whole(chip_at(d) * 2 + 1 - core).astype(BF16)
                sib_copy(2, d).start()

            send_later(0, 8, functools.partial(sib_copy, 2))

        elif e in ("xa", "xf"):
            spread_x(0 if e == "xa" else 2)
        elif e in ("ca", "cf"):
            cross(0 if e == "ca" else 2)
        elif e == "xb":
            spread(1)
        elif e in ("na", "nb"):
            sums, samples = (near_ca, all_a) if e == "na" else (near_cb, all_b)
            sums[0] = jnp.zeros((32, LEAF), F32)

            @pl.loop(0, NEAR_MOST // 16)
            def _(g):
                for u in range(16):
                    s = g * 16 + u
                    sums[s + 1] = sums[index[2, s]] + dot_n(samples[index[1, s]], near_k[s])

        elif e in ("sa", "sb"):
            h = "ab".index(e[1])

            @pl.loop(0, 8)
            def _(i):
                d = 7 - i
                owner = chip_at(d) * 2 + 1 - core
                for k in range(4):
                    near_out[h, d, :, k * LEAF : (k + 1) * LEAF] = near_leaf(h, owner, k).astype(BF16)
                sib_copy(h, d).start()

            send_later(0, 8, functools.partial(sib_copy, h))
        elif e == "ef":
            sib_copy(2, 0).wait_recv()
            total = far_whole(c) + far_sib[0].astype(F32)
            for d in range(1, 5):
                chip_copy(2, d).wait_recv()
                total = total + far_in[d].astype(F32)
            middle = total[:, 256:384] + split_dot(total[:, 384:448], moves_t[:, 256:384])
            for k in range(4):
                leaf = total[:, k * 64 : (k + 1) * 64] + split_dot(
                    middle[:, (k // 2) * 64 : (k // 2) * 64 + 64], moves_t[:, k * 64 : (k + 1) * 64]
                )
                lanes = slice(k * LEAF, (k + 1) * LEAF)
                far_part[:, lanes] = split_dot(leaf, basis_t[:, lanes])
        elif e in ("ea", "eb"):
            h = "ab".index(e[1])
            rows = slice(32 * h, 32 * h + 32)
            sib_copy(h, 0).wait_recv()
            others = range(1, 5) if h == 0 else range(1, 8)
            for d in others:
                chip_copy(h, d).wait_recv()
            for k in range(4):
                lanes = slice(k * LEAF, (k + 1) * LEAF)
                total = near_leaf(h, c, k) + near_sib[h, 0, :, lanes].astype(F32) + far_part[rows, lanes]
                for d in others:
                    total = total + near_in[h, d, :, lanes].astype(F32)
                out[rows, lanes] = total.astype(BF16)
            stores[h].start()
        elif e == "T":
            loads["near"].wait()
            loads["far"].wait()
            index_v[...], weight_v[...] = slot_tables(
                near_list[...], near_count[0, 0], far_list[...], far_count[0, 0]
            )
            for one in tables:
                one.start()
        elif e == "W":
            for one in tables:
                one.wait()
        else:
            raise ValueError(e)

    def store_features(leaf, skel, d, feat):
        leaf[pl.ds(d * 4, 4)] = feat[:, 0:256].reshape(4, 16, 256)
        skel[pl.ds(d * 4, 4)] = feat[:, 256:384].reshape(4, 16, 128)

    def one_of(pair, first, second):
        pair = pair.astype(F32)
        return (pair[:, :64] * first + pair[:, 64:] * second).astype(BF16)

    for e in order:
        event(e)

    for one in unsent:
        one()
    for one in stores:
        one.wait()


def run(near_count, far_count, near_list, far_list, sel, points, skeleton, probes_t, basis_t, moves_t):
    smem = pl.BlockSpec(memory_space=pltpu.SMEM)
    dma = pltpu.SemaphoreType.DMA
    return pl.pallas_call(
        functools.partial(main_kernel, ORDER),
        out_shape=jax.ShapeDtypeStruct((64, 1024), BF16),
        in_specs=[smem] * 2 + [pl.BlockSpec(memory_space=pl.ANY)] * 8,
        out_specs=pl.BlockSpec(memory_space=pl.ANY),
        scratch_shapes=[
            pltpu.VMEM((2, NEAR_MOST), jnp.int32),
            pltpu.VMEM((2, FAR_MOST), jnp.int32),
            pltpu.VMEM((128, 32), BF16),
            pltpu.VMEM((3, 4 * LEAF), BF16),
            pltpu.VMEM((3, 7 * RANK), BF16),
            pltpu.VMEM((64, 4 * LEAF), BF16),
            pltpu.VMEM((64, 6 * RANK), BF16),
            pltpu.VMEM((64, 4 * LEAF), BF16),
            dma((15,)),
            dma((2,)),
            pltpu.VMEM((16, GEO), BF16),
            pltpu.VMEM((8, 128), jnp.int32),
            pltpu.SMEM((8, 128), jnp.int32),
            pltpu.VMEM((8, 128), F32),
            pltpu.SMEM((8, 128), F32),
            dma((2,)),
            pltpu.VMEM((4 * N_ROW, 32, LEAF), BF16),
            pltpu.VMEM((4 * N_ROW, 32, LEAF), BF16),
            pltpu.VMEM((8 * N_ROW, 32, 128), BF16),
            pltpu.VMEM((N_Y, N_ZH, 16, GEO), BF16),
            pltpu.VMEM((N_COL, 16, GEO), BF16),
            pltpu.VMEM((4 * N_ROW, 16, LEAF), BF16),
            pltpu.VMEM((4 * N_COL, 16, LEAF), BF16),
            pltpu.VMEM((4 * N_ROW, 16, 128), BF16),
            pltpu.VMEM((4 * N_COL, 16, 128), BF16),
            pltpu.VMEM((NEAR_MOST, LEAF, LEAF), BF16),
            pltpu.VMEM((FAR_MOST, 2 * RANK, RANK), BF16),
            pltpu.VMEM((NEAR_MOST + 1, 32, LEAF), F32),
            pltpu.VMEM((NEAR_MOST + 1, 32, LEAF), F32),
            pltpu.VMEM((FAR_MOST + 1, SAMPLES, RANK), F32),
            pltpu.VMEM((2, 8, 32, 1024), BF16),
            pltpu.VMEM((8, 64, 512), BF16),
            pltpu.VMEM((2, 8, 32, 1024), BF16),
            pltpu.VMEM((8, 64, 512), BF16),
            pltpu.VMEM((2, 8, 32, 1024), BF16),
            pltpu.VMEM((8, 64, 512), BF16),
            pltpu.VMEM((2, 8, 32, 1024), BF16),
            pltpu.VMEM((8, 64, 512), BF16),
            pltpu.VMEM((64, 1024), F32),
            dma((120,)),
            dma((N_ROW, 2)),
            dma((N_ROW, 2)),
            dma((N_ROW, 2)),
            dma((4,)),
            dma((4,)),
            dma((2, N_COL)),
            dma((2, 4)),
            dma((2, 4)),
            dma((6, 8)),
            dma((6, 8)),
        ],
        compiler_params=pltpu.CompilerParams(
            collective_id=0, has_side_effects=True, vmem_limit_bytes=56 << 20
        ),
        name="sample",
    )(near_count, far_count, near_list, far_list, sel, points, skeleton, probes_t, basis_t, moves_t)


def local(
    probes, points, skeleton, leaf_basis, transfer, near_list, near_count, far_list, far_count
):
    sel = jnp.asarray(selections(), BF16)
    return run(
        near_count, far_count, near_list[0, 0], far_list[0, 0],
        sel, points, skeleton, probes.T, leaf_basis.T, transfer.T,
    ).T


def solution(mesh):
    placed = (
        P(("row", "col"), None),
        P(None, ("row", "col")),
        P(None, ("row", "col")),
        P(("row", "col"), None),
        P(("row", "col"), None),
        P("row", "col", None, None),
        P("row", "col"),
        P("row", "col", None, None),
        P("row", "col"),
    )
    return jax.shard_map(
        local, mesh=mesh, in_specs=placed, out_specs=P(("row", "col"), None), check_vma=False
    )
```

```python
import functools
import math

import jax
import jax.numpy as jnp
import numpy as np
from jax import lax
from jax.experimental import pallas as pl
from jax.experimental.pallas import tpu as pltpu
from jax.sharding import PartitionSpec as P

LEAF = 256
RANK = 64
SAMPLES = 64
N_ROW = 32
N_COL = 16
N_Y = 8
N_ZH = 4
NEAR_MOST = 64
FAR_MOST = 128
GEO = 384
MESH = pl.DeviceIdType.MESH
F32 = jnp.float32
BF16 = jnp.bfloat16
RATE = math.sqrt(3.0) / 0.15
RATE2 = RATE * math.log2(math.e)


def dot_t(a, b):
    return lax.dot_general(a, b, (((1,), (1,)), ((), ())), preferred_element_type=F32)


def dot_l(a, b):
    return lax.dot_general(a, b, (((0,), (0,)), ((), ())), preferred_element_type=F32)


def dot_n(a, b):
    return jnp.dot(a, b, preferred_element_type=F32)


def selections():
    col = np.zeros((4, 16, 32), np.float32)
    row = np.zeros((4, 16, 32), np.float32)
    for k in range(4):
        for i in range(3):
            col[k, i, i * 4 + k] = -2.0
            row[k, i, i * 4 + k] = 1.0
            col[k, 3 + i, 16 + 4 * i + k] = 1.0
            row[k, 3 + i, 28] = 1.0
            col[k, 6 + i, 28] = 1.0
            row[k, 6 + i, 16 + 4 * i + k] = 1.0
    return np.concatenate([col.reshape(64, 32), row.reshape(64, 32)], axis=0)


def upward_packet(probes_t, basis_t, moves_t):
    leaves = [
        dot_t(probes_t[:, k * LEAF : (k + 1) * LEAF], basis_t[:, k * LEAF : (k + 1) * LEAF])
        for k in range(4)
    ]
    leaf = jnp.concatenate(leaves, axis=1).astype(BF16)
    mids = [
        dot_t(leaf[:, j * 128 : (j + 1) * 128], moves_t[:, j * 128 : (j + 1) * 128])
        for j in range(2)
    ]
    mid = jnp.concatenate(mids, axis=1).astype(BF16)
    top = dot_t(mid, moves_t[:, 256:384]).astype(BF16)
    halves = jnp.concatenate([top[:32], top[32:]], axis=1)
    halves = jnp.concatenate([halves, halves], axis=0)
    return jnp.concatenate([leaf, mid, halves], axis=1)


def matern(square):
    square = jnp.maximum(square, 1e-30)
    dist = square * lax.rsqrt(square)
    return (1.0 + RATE * dist) * jnp.exp2(dist * (-RATE2))


def split_dot(a, b):
    high = a.astype(BF16)
    low = (a - high.astype(F32)).astype(BF16)
    both = dot_n(jnp.concatenate([high, low], axis=0), b)
    return both[: a.shape[0]] + both[a.shape[0] :]


def features(sel, geo):
    flat = geo.astype(F32)
    squares = flat * flat
    norm = squares[0:4] + squares[4:8] + squares[8:12]
    high = norm.astype(BF16).astype(F32)
    rest = norm - high
    middle = rest.astype(BF16).astype(F32)
    low = rest - middle
    stack = jnp.concatenate([flat, high, middle, low, jnp.ones_like(norm)], axis=0)
    return dot_n(sel, stack.astype(BF16)).astype(BF16)


def packed(points, skeleton):
    pts = points.astype(F32)
    skel = skeleton.astype(F32)
    rows = []
    for i in range(3):
        for k in range(4):
            tail = skel[i : i + 1, k * 128 : min(k * 128 + 128, 448)]
            if k == 3:
                tail = jnp.concatenate([tail, jnp.zeros((1, 64), F32)], axis=1)
            rows.append(jnp.concatenate([pts[i : i + 1, k * LEAF : (k + 1) * LEAF], tail], axis=1))
    rows.append(jnp.zeros((4, GEO), F32))
    return jnp.concatenate(rows, axis=0).astype(BF16)


def chain(targets, live):
    across = jnp.broadcast_to(targets, (128, 128))
    down = across.T
    row = lax.broadcasted_iota(jnp.int32, (128, 128), 0)
    lane = lax.broadcasted_iota(jnp.int32, (128, 128), 1)
    prev = jnp.where((across == down) & (row < lane), row + 1, 0)
    last = jnp.where((down == lane) & (row < live), row + 1, 0)
    return jnp.max(prev, axis=0, keepdims=True), jnp.max(last, axis=0, keepdims=True)


def slot_tables(near_list, near_live, far_list, far_live):
    near = jnp.concatenate([near_list, jnp.zeros((2, 64), jnp.int32)], axis=1)
    target = jnp.clip(near[0:1], 0, 4 * N_COL - 1)
    source = jnp.clip(near[1:2], 0, 4 * N_ROW - 1)
    far_target = jnp.clip(far_list[0:1], 0, 7 * N_COL - 1)
    far_source = jnp.clip(far_list[1:2], 0, 7 * N_ROW - 1)
    far = jnp.concatenate([far_target, far_source], axis=0)
    device = (far * 9363) >> 16
    local = far - device * 7
    half = local >> 1
    odd = (local - half * 2).astype(F32)
    place = device * 4 + half
    index = jnp.concatenate(
        [target, source, *chain(target, near_live), place, *chain(far_target, far_live)], axis=0
    )
    weights = jnp.concatenate([1.0 - odd[0:1], odd[0:1], 1.0 - odd[1:2], odd[1:2]], axis=0)
    return index, jnp.concatenate([weights, jnp.zeros((4, 128), F32)], axis=0)


ORDER = (
    "pk", "g0", "a0", "b0", "up", "q0", "gz", "a10", "q10", "gy1", "qz1", "by1", "gy2", "q13", "gr", "qz2", "bz0",
    "T", "by2", "gy3", "q11", "q20", "q12", "az1", "gy4", "W", "F0", "by3", "F1", "q23", "q21", "K1", "q22", "N0",
    "K0", "az2", "N7", "N4", "q30", "N5", "a11", "bz1", "N1", "N3", "q33", "q31", "bz2", "q32", "bz3", "a12",
    "a13", "by4", "K3", "K2", "a20", "a21", "q43", "N6", "q42", "q40", "q41", "U", "M0", "a22", "M1", "a23", "M2",
    "M3", "a30", "fs", "a31", "xf", "a32", "a33", "bz4", "N2", "a41", "a40", "a43", "a42", "na", "sa", "be", "nb",
    "xa", "sb", "cf", "xb", "ca", "sw", "ef", "ea", "eb",
)


def main_kernel(
    order,
    near_count, far_count, near_any, far_any, sel_any, points_any, skeleton_any, probes_any, basis_any,
    moves_any,
    out_any,
    near_list, far_list, sel, points, skeleton, basis_t, moves_t, out, in_sems, out_sems,
    geo, index_v, index, weight_v, weight, table_sems,
    all_a, all_b, all_q, col_geo, row_geo, col_leaf, row_leaf, col_skel, row_skel,
    near_k, far_k, near_ca, near_cb, far_c, near_out, far_out,
    near_sib, far_sib, near_sum, far_sum, near_in, far_in, far_part,
    send, recv_a, recv_b, recv_q, geo_send, geo_recv, row_sems, ring_send, ring_recv, sems, sib_sems,
):
    r = lax.axis_index("row")
    c = lax.axis_index("col")
    zh = lax.div(r, N_Y)
    y = lax.rem(r, N_Y)
    core = lax.rem(c, 2)
    chip = lax.div(c, 2)
    sibling = chip * 2 + 1 - core
    z_lo = lax.div(chip, 4)
    x = lax.rem(chip, 4)

    def slot(dz, dy):
        return lax.rem(zh + dz, N_ZH) * N_Y + lax.rem(y + dy % N_Y, N_Y)

    up, down, across = slot(1, 0), slot(3, 0), slot(2, 0)
    right, left = slot(0, 1), slot(0, -1)
    me = slot(0, 0)

    barrier = pltpu.get_barrier_semaphore()
    for row in (up, down, across, right, left):
        pl.semaphore_signal(barrier, inc=1, device_id=(row, c), device_id_type=MESH)

    @pl.loop(1, N_COL)
    def _(d):
        pl.semaphore_signal(
            barrier, inc=1, device_id=(r, (c + d) % N_COL), device_id_type=MESH
        )

    loads = {
        name: pltpu.make_async_copy(src, dst, in_sems.at[i])
        for i, (name, src, dst) in enumerate(
            (
                ("points", points_any, points),
                ("skeleton", skeleton_any, skeleton),
                ("basis", basis_any, basis_t),
                ("moves", moves_any, moves_t),
                ("near", near_any, near_list),
                ("far", far_any, far_list),
                ("sel", sel_any, sel),
            )
        )
    }
    own = []
    for h, buf in enumerate((all_a, all_b)):
        for k in range(4):
            piece = probes_any.at[pl.ds(32 * h, 32), pl.ds(k * LEAF, LEAF)]
            own.append(pltpu.make_async_copy(piece, buf.at[me * 4 + k], in_sems.at[7 + 4 * h + k]))
    for one in own:
        one.start()
    for one in loads.values():
        one.start()
    for one in own:
        one.wait()
    pl.semaphore_wait(barrier, 5 + N_COL - 1)

    sends = []
    started = []
    unsent = []
    gathered = []

    def send_later(first, last, copy_of, held=unsent):
        def waits():
            @pl.loop(first, last)
            def _(d):
                copy_of(d).wait_send()

        held.append(waits)

    def copy(src, dst, sem, row):
        one = pltpu.make_async_remote_copy(
            src_ref=src, dst_ref=dst, send_sem=send.at[len(started)], recv_sem=sem,
            device_id=(row, c), device_id_type=MESH,
        )
        one.start()
        sends.append(one)
        started.append(one)

    def arrived(dst, sem):
        pltpu.make_async_remote_copy(
            src_ref=dst, dst_ref=dst, send_sem=send.at[0], recv_sem=sem,
            device_id=(right, c), device_id_type=MESH,
        ).wait_recv()

    def mover(buf, sems, pitch, parts):
        def block(s, h=None):
            at = 0 if h != 1 else parts[0]
            return buf.at[pl.ds(s * pitch + at, sum(parts) if h is None else parts[h])]

        def push(s, row, h=None):
            copy(block(s, h), block(s, h), sems.at[s, h or 0], row)

        def wait(s, h=None):
            arrived(block(s, h), sems.at[s, h or 0])

        return push, wait

    movers = {
        "a": mover(all_a, recv_a, 4, (2, 2)),
        "b": mover(all_b, recv_b, 4, (2, 2)),
        "q": mover(all_q, recv_q, 8, (4, 3)),
    }

    def ring(name, dz, k):
        push, wait = movers[name]
        if k == 4:
            wait(slot(dz, 4), 0)
            wait(slot(dz, 4), 1)
            return
        wait(slot(dz, -k))
        push(slot(dz, -k), right, 0 if k == 3 else None)
        wait(slot(dz, k))
        push(slot(dz, k), left, 1 if k == 3 else None)

    def turn(name, dy):
        push, wait = movers[name]
        wait(slot(3, dy))
        push(slot(3, dy), up, 0)
        wait(slot(1, dy))
        push(slot(1, dy), down, 1)

    def geo_z(d):
        return pltpu.make_async_remote_copy(
            src_ref=geo, dst_ref=col_geo.at[y, zh],
            send_sem=geo_send.at[d], recv_sem=geo_recv.at[d],
            device_id=(slot(d, 0), c), device_id_type=MESH,
        )

    def geo_y(k, way):
        place = (y - k) % N_Y if way == 0 else (y + k) % N_Y
        return pltpu.make_async_remote_copy(
            src_ref=col_geo.at[place], dst_ref=col_geo.at[place],
            send_sem=ring_send.at[way, k], recv_sem=ring_recv.at[way, k],
            device_id=(right if way == 0 else left, c), device_id_type=MESH,
        )

    def geo_y_wait(k, way):
        place = (y - k - 1) % N_Y if way == 0 else (y + k + 1) % N_Y
        arrived(col_geo.at[place], ring_recv.at[way, k])

    def geo_row(d):
        return pltpu.make_async_remote_copy(
            src_ref=geo, dst_ref=row_geo.at[c],
            send_sem=row_sems.at[0, d], recv_sem=row_sems.at[1, d],
            device_id=(r, (c + d) % N_COL), device_id_type=MESH,
        )

    outs = (near_out.at[0], near_out.at[1], far_out)
    sibs = (near_sib.at[0], near_sib.at[1], far_sib)
    whole = (near_sum.at[0], near_sum.at[1], far_sum)
    comes = (near_in.at[0], near_in.at[1], far_in)

    def sib_copy(what, d):
        return pltpu.make_async_remote_copy(
            src_ref=outs[what].at[d], dst_ref=sibs[what].at[d],
            send_sem=sib_sems.at[2 * what, d], recv_sem=sib_sems.at[2 * what + 1, d],
            device_id=(r, sibling), device_id_type=MESH,
        )

    def chip_at(d):
        return lax.rem(z_lo + lax.div(d, 4), 2) * 4 + lax.rem(x + lax.rem(d, 4), 4)

    def chip_copy(what, d, by_x=False):
        to = chip_at(lax.rem(d, 4) if by_x else d)
        return pltpu.make_async_remote_copy(
            src_ref=whole[what].at[d], dst_ref=comes[what].at[d],
            send_sem=sems.at[2 * what, d], recv_sem=sems.at[2 * what + 1, d],
            device_id=(r, to * 2 + core), device_id_type=MESH,
        )

    def core_sum(what, d):
        sib_copy(what, d).wait_recv()
        owner = chip_at(d) * 2 + core
        if what == 2:
            far_sum[d] = (far_whole(owner) + far_sib[d].astype(F32)).astype(BF16)
            return
        for k in range(4):
            lanes = slice(k * LEAF, (k + 1) * LEAF)
            theirs = near_sib[what, d, :, lanes].astype(F32)
            near_sum[what, d, :, lanes] = (near_leaf(what, owner, k) + theirs).astype(BF16)

    def spread(what):
        @pl.loop(0, 7)
        def _(i):
            core_sum(what, 7 - i)
            chip_copy(what, 7 - i).start()

        send_later(1, 8, functools.partial(chip_copy, what))

    def spread_x(what):
        for first in (5, 1):

            @pl.loop(0, 3)
            def _(i):
                d = first + 2 - i
                core_sum(what, d)
                chip_copy(what, d, True).start()

            send_later(first, first + 3, functools.partial(chip_copy, what, by_x=True))

        core_sum(what, 4)

    def cross(what):
        total = whole[what][4].astype(F32)
        for d in (5, 6, 7):
            chip_copy(what, d, True).wait_recv()
            total = total + comes[what][d].astype(F32)
        whole[what][4] = total.astype(BF16)
        chip_copy(what, 4).start()
        send_later(4, 5, functools.partial(chip_copy, what))

    def near_leaf(h, owner, k):
        return (near_ca, near_cb)[h][index[3, owner * 4 + k]]

    def far_whole(owner):
        parts = [far_c[index[7, owner * 7 + j]] for j in range(7)] + [jnp.zeros((64, 64), F32)]
        return jnp.concatenate(parts, axis=1)

    stores = [
        pltpu.make_async_copy(
            out.at[pl.ds(32 * h, 32)], out_any.at[pl.ds(32 * h, 32)], out_sems.at[h]
        )
        for h in range(2)
    ]
    tables = (
        pltpu.make_async_copy(index_v, index, table_sems.at[0]),
        pltpu.make_async_copy(weight_v, weight, table_sems.at[1]),
    )

    def event(e):
        if e == "pk":
            loads["points"].wait()
            loads["skeleton"].wait()
            geo[...] = packed(points[...], skeleton[...])
            col_geo[y, zh] = geo[...]
            row_geo[c] = geo[...]
        elif e == "sw":
            while sends:
                sends.pop().wait_send()
            while gathered:
                gathered.pop()()
        elif e == "g0":
            for d in (1, 2, 3):
                geo_z(d).start()

            @pl.loop(1, N_COL)
            def _(d):
                geo_row(d).start()

            send_later(1, 4, geo_z, gathered)
            send_later(1, N_COL, geo_row, gathered)

        elif e == "up":
            loads["basis"].wait()
            loads["moves"].wait()
            probes_t = jnp.concatenate(
                [
                    jnp.concatenate([buf[me * 4 + k] for k in range(4)], axis=1)
                    for buf in (all_a, all_b)
                ],
                axis=0,
            )
            packet = upward_packet(probes_t, basis_t[...], moves_t[...])
            for j in range(7):
                rows = slice((j % 2) * 32, (j % 2) * 32 + 32)
                all_q[me * 8 + j] = packet[rows, (j // 2) * 128 : (j // 2) * 128 + 128]
        elif e in ("a0", "b0", "q0"):
            for row in (right, left, up, down) if e == "b0" else (up, down, right, left):
                movers[e[0]][0](me, row)
        elif e == "gz":
            for d in (1, 2, 3):
                arrived(col_geo.at[y, (zh - d) % N_ZH], geo_recv.at[d])
            geo_y(0, 0).start()
            geo_y(0, 1).start()
            send_later(0, 4, lambda k: geo_y(k, 0), gathered)
            send_later(0, 3, lambda k: geo_y(k, 1), gathered)
        elif e in ("gy1", "gy2", "gy3", "gy4"):
            k = int(e[2])
            geo_y_wait(k - 1, 0)
            if k < 4:
                geo_y(k, 0).start()
                geo_y_wait(k - 1, 1)
                if k < 3:
                    geo_y(k, 1).start()
        elif e in ("az1", "qz1"):
            turn(e[0], 0)
            for dz in (3, 1):
                movers[e[0]][0](slot(dz, 0), right)
                movers[e[0]][0](slot(dz, 0), left)
        elif e in ("az2", "qz2"):
            push, wait = movers[e[0]]
            wait(slot(2, 0), 0)
            wait(slot(2, 0), 1)
            push(slot(2, 0), right)
            push(slot(2, 0), left)
        elif e[0] in "aq":
            ring(e[0], int(e[2]), int(e[1]))
        elif e[:2] == "by":
            k = int(e[2])
            ring("b", 0, k)
            for dy in (-k, k) if k < 4 else (4,):
                movers["b"][0](slot(0, dy), up)
                movers["b"][0](slot(0, dy), down)
        elif e[:2] == "bz":
            k = int(e[2])
            for dy in (-k, k) if 0 < k < 4 else (k,):
                turn("b", dy)
        elif e == "be":
            for dy in (0, -1, 1, -2, 2, -3, 3, 4):
                movers["b"][1](slot(2, dy), 0)
                movers["b"][1](slot(2, dy), 1)
        elif e == "gr":

            @pl.loop(1, N_COL)
            def _(d):
                arrived(row_geo.at[(c + N_COL - d) % N_COL], row_sems.at[1, d])

        elif e[0] == "F":
            part = int(e[1])
            if part == 0:
                loads["sel"].wait()

            @pl.loop(part * 4, part * 4 + 4)
            def _(j):
                wide = jnp.concatenate([col_geo[j, k] for k in range(N_ZH)], axis=1)
                feat = features(sel[0:64], wide)
                for k in range(N_ZH):
                    store_features(col_leaf, col_skel, k * N_Y + j, feat[:, k * GEO : (k + 1) * GEO])

            @pl.loop(part * 2, part * 2 + 2)
            def _(j):
                wide = jnp.concatenate([row_geo[j * 4 + k] for k in range(4)], axis=1)
                feat = features(sel[64:128], wide)
                for k in range(4):
                    store_features(row_leaf, row_skel, j * 4 + k, feat[:, k * GEO : (k + 1) * GEO])

        elif e[0] == "N":
            for u in range(8):
                s = int(e[1]) * 8 + u
                square = dot_l(col_leaf[index[1, s]], row_leaf[index[0, s]])
                near_k[s] = matern(square).astype(BF16)
        elif e[0] == "K":

            @pl.loop(int(e[1]) * 2, int(e[1]) * 2 + 2)
            def _(g):
                for u in range(16):
                    s = g * 16 + u
                    ours = one_of(col_skel[index[5, s]], weight[2, s], weight[3, s])
                    theirs = one_of(row_skel[index[4, s]], weight[0, s], weight[1, s])
                    kern = matern(dot_l(ours, theirs))
                    far_k[s, 0:64] = (kern * weight[2, s]).astype(BF16)
                    far_k[s, 64:128] = (kern * weight[3, s]).astype(BF16)

        elif e == "U":
            far_c[0] = jnp.zeros((64, 64), F32)

            @pl.loop(0, N_ROW // 4)
            def _(g):
                for u in range(4):
                    d = g * 4 + u
                    top = all_q[d * 8 + 6]
                    all_q[d * 8 + 7] = jnp.concatenate([top[:, 64:], top[:, :64]], axis=1)

        elif e[0] == "M":

            @pl.loop(int(e[1]) * 2, int(e[1]) * 2 + 2)
            def _(g):
                for u in range(16):
                    s = g * 16 + u
                    at = index[5, s] * 2
                    pair = jnp.concatenate([all_q[at], all_q[at + 1]], axis=0)
                    far_c[s + 1] = far_c[index[6, s]] + dot_n(pair, far_k[s])

        elif e == "fs":

            @pl.loop(0, 8)
            def _(i):
                d = 7 - i
                far_out[d] = far_whole(chip_at(d) * 2 + 1 - core).astype(BF16)
                sib_copy(2, d).start()

            send_later(0, 8, functools.partial(sib_copy, 2))

        elif e in ("xa", "xf"):
            spread_x(0 if e == "xa" else 2)
        elif e in ("ca", "cf"):
            cross(0 if e == "ca" else 2)
        elif e == "xb":
            spread(1)
        elif e in ("na", "nb"):
            sums, samples = (near_ca, all_a) if e == "na" else (near_cb, all_b)
            sums[0] = jnp.zeros((32, LEAF), F32)

            @pl.loop(0, NEAR_MOST // 16)
            def _(g):
                for u in range(16):
                    s = g * 16 + u
                    sums[s + 1] = sums[index[2, s]] + dot_n(samples[index[1, s]], near_k[s])

        elif e in ("sa", "sb"):
            h = "ab".index(e[1])

            @pl.loop(0, 8)
            def _(i):
                d = 7 - i
                owner = chip_at(d) * 2 + 1 - core
                for k in range(4):
                    near_out[h, d, :, k * LEAF : (k + 1) * LEAF] = near_leaf(h, owner, k).astype(BF16)
                sib_copy(h, d).start()

            send_later(0, 8, functools.partial(sib_copy, h))
        elif e == "ef":
            sib_copy(2, 0).wait_recv()
            total = far_whole(c) + far_sib[0].astype(F32)
            for d in range(1, 5):
                chip_copy(2, d).wait_recv()
                total = total + far_in[d].astype(F32)
            middle = total[:, 256:384] + split_dot(total[:, 384:448], moves_t[:, 256:384])
            for k in range(4):
                leaf = total[:, k * 64 : (k + 1) * 64] + split_dot(
                    middle[:, (k // 2) * 64 : (k // 2) * 64 + 64], moves_t[:, k * 64 : (k + 1) * 64]
                )
                lanes = slice(k * LEAF, (k + 1) * LEAF)
                far_part[:, lanes] = split_dot(leaf, basis_t[:, lanes])
        elif e in ("ea", "eb"):
            h = "ab".index(e[1])
            rows = slice(32 * h, 32 * h + 32)
            sib_copy(h, 0).wait_recv()
            others = range(1, 5) if h == 0 else range(1, 8)
            for d in others:
                chip_copy(h, d).wait_recv()
            for k in range(4):
                lanes = slice(k * LEAF, (k + 1) * LEAF)
                total = near_leaf(h, c, k) + near_sib[h, 0, :, lanes].astype(F32) + far_part[rows, lanes]
                for d in others:
                    total = total + near_in[h, d, :, lanes].astype(F32)
                out[rows, lanes] = total
            stores[h].start()
        elif e == "T":
            loads["near"].wait()
            loads["far"].wait()
            index_v[...], weight_v[...] = slot_tables(
                near_list[...], near_count[0, 0], far_list[...], far_count[0, 0]
            )
            for one in tables:
                one.start()
        elif e == "W":
            for one in tables:
                one.wait()
        else:
            raise ValueError(e)

    def store_features(leaf, skel, d, feat):
        leaf[pl.ds(d * 4, 4)] = feat[:, 0:256].reshape(4, 16, 256)
        skel[pl.ds(d * 4, 4)] = feat[:, 256:384].reshape(4, 16, 128)

    def one_of(pair, first, second):
        pair = pair.astype(F32)
        return (pair[:, :64] * first + pair[:, 64:] * second).astype(BF16)

    for e in order:
        event(e)

    for one in unsent:
        one()
    for one in stores:
        one.wait()


def run(near_count, far_count, near_list, far_list, sel, points, skeleton, probes_t, basis_t, moves_t):
    smem = pl.BlockSpec(memory_space=pltpu.SMEM)
    dma = pltpu.SemaphoreType.DMA
    return pl.pallas_call(
        functools.partial(main_kernel, ORDER),
        out_shape=jax.ShapeDtypeStruct((64, 1024), F32),
        in_specs=[smem] * 2 + [pl.BlockSpec(memory_space=pl.ANY)] * 8,
        out_specs=pl.BlockSpec(memory_space=pl.ANY),
        scratch_shapes=[
            pltpu.VMEM((2, NEAR_MOST), jnp.int32),
            pltpu.VMEM((2, FAR_MOST), jnp.int32),
            pltpu.VMEM((128, 32), BF16),
            pltpu.VMEM((3, 4 * LEAF), BF16),
            pltpu.VMEM((3, 7 * RANK), BF16),
            pltpu.VMEM((64, 4 * LEAF), BF16),
            pltpu.VMEM((64, 6 * RANK), BF16),
            pltpu.VMEM((64, 4 * LEAF), F32),
            dma((15,)),
            dma((2,)),
            pltpu.VMEM((16, GEO), BF16),
            pltpu.VMEM((8, 128), jnp.int32),
            pltpu.SMEM((8, 128), jnp.int32),
            pltpu.VMEM((8, 128), F32),
            pltpu.SMEM((8, 128), F32),
            dma((2,)),
            pltpu.VMEM((4 * N_ROW, 32, LEAF), BF16),
            pltpu.VMEM((4 * N_ROW, 32, LEAF), BF16),
            pltpu.VMEM((8 * N_ROW, 32, 128), BF16),
            pltpu.VMEM((N_Y, N_ZH, 16, GEO), BF16),
            pltpu.VMEM((N_COL, 16, GEO), BF16),
            pltpu.VMEM((4 * N_ROW, 16, LEAF), BF16),
            pltpu.VMEM((4 * N_COL, 16, LEAF), BF16),
            pltpu.VMEM((4 * N_ROW, 16, 128), BF16),
            pltpu.VMEM((4 * N_COL, 16, 128), BF16),
            pltpu.VMEM((NEAR_MOST, LEAF, LEAF), BF16),
            pltpu.VMEM((FAR_MOST, 2 * RANK, RANK), BF16),
            pltpu.VMEM((NEAR_MOST + 1, 32, LEAF), F32),
            pltpu.VMEM((NEAR_MOST + 1, 32, LEAF), F32),
            pltpu.VMEM((FAR_MOST + 1, SAMPLES, RANK), F32),
            pltpu.VMEM((2, 8, 32, 1024), BF16),
            pltpu.VMEM((8, 64, 512), BF16),
            pltpu.VMEM((2, 8, 32, 1024), BF16),
            pltpu.VMEM((8, 64, 512), BF16),
            pltpu.VMEM((2, 8, 32, 1024), BF16),
            pltpu.VMEM((8, 64, 512), BF16),
            pltpu.VMEM((2, 8, 32, 1024), BF16),
            pltpu.VMEM((8, 64, 512), BF16),
            pltpu.VMEM((64, 1024), F32),
            dma((120,)),
            dma((N_ROW, 2)),
            dma((N_ROW, 2)),
            dma((N_ROW, 2)),
            dma((4,)),
            dma((4,)),
            dma((2, N_COL)),
            dma((2, 4)),
            dma((2, 4)),
            dma((6, 8)),
            dma((6, 8)),
        ],
        compiler_params=pltpu.CompilerParams(
            collective_id=0, has_side_effects=True, vmem_limit_bytes=56 << 20
        ),
        name="sample",
    )(near_count, far_count, near_list, far_list, sel, points, skeleton, probes_t, basis_t, moves_t)


def local(
    probes, points, skeleton, leaf_basis, transfer, near_list, near_count, far_list, far_count
):
    sel = jnp.asarray(selections(), BF16)
    return run(
        near_count, far_count, near_list[0, 0], far_list[0, 0],
        sel, points, skeleton, probes.T, leaf_basis.T, transfer.T,
    ).astype(BF16).T


def solution(mesh):
    placed = (
        P(("row", "col"), None),
        P(None, ("row", "col")),
        P(None, ("row", "col")),
        P(("row", "col"), None),
        P(("row", "col"), None),
        P("row", "col", None, None),
        P("row", "col"),
        P("row", "col", None, None),
        P("row", "col"),
    )
    return jax.shard_map(
        local, mesh=mesh, in_specs=placed, out_specs=P(("row", "col"), None), check_vma=False
    )
```
